256 devices in a mesh: gx: 8 (over x, core), gy: 16 (over z, y_lo), gz: 2 (over y_hi).
Axes of the slice: x: 4, y: 4 (y_hi: 2, y_lo: 2; y = y_hi * 2 + y_lo), z: 8, core: 2. Of those that a mesh axis runs over, the one named last changes fastest.
Arguments:
- velocity: float32 [3, 2, 4096, 4096], P(None, 'gz', 'gx', 'gy'), may hold values from -6 to 6
Outputs:
- divergence: float32 [3, 2, 4096, 4096], P(None, 'gz', 'gx', 'gy')
- coefficient: float32 [2], replicated
The draws below stay inside these ranges and needn't reach their ends.
All inputs are finite; a program needn't handle non-finite values.
Results may differ from the reference program's by a relative error of at most 0.0003.
Values sent between devices are 32-bit elements; how exact they have to be, the bound alone decides.
No kernel may reach another device: no remote copies, remote signals or barrier semaphores. Data moves between devices by JAX's collectives and lax.ppermute only.
A program may use at most 128 MiB of HBM per device.

```python
import jax
import jax.numpy as jnp
from jax import lax

NX = 4096
NY = 4096
NZ = 2


def levels(rng, dims, split, smallest, high):
    loudness, own = 1.0, jax.random.fold_in(rng, 6)
    for axis_at, shards_of in split:
        steps = jnp.exp(jax.random.uniform(jax.random.fold_in(own, axis_at), (shards_of,), jnp.float32, smallest / len(split), high / len(split)))
        loudness = loudness * jnp.repeat(steps, dims[axis_at] // shards_of).reshape([-1 if axis == axis_at else 1 for axis in range(len(dims))])
    return loudness


def noise(key, extent, deviation, reach, cuts=(), kind=jnp.bfloat16):
    drawn = jax.random.normal(key, extent, jnp.float32) * deviation
    if len(cuts) > 0:
        drawn = levels(key, extent, cuts, -0.22, 0.18) * drawn
    return jnp.clip(drawn, min=-reach, max=reach).astype(kind)


def setup_inputs(seed: int = 0) -> dict:
    seeds = jax.random.split(jax.random.key(seed), 2)
    velocity = noise(seeds[0], (3, NZ, NX, NY), 1.0, 6.0, ((1, 2), (2, 8), (3, 16)), jnp.float32)
    return dict(velocity=velocity)


def filter_symbol(cells):
    wave = 2.0 * jnp.pi * jnp.arange(cells // 2 + 1, dtype=jnp.float32) / cells
    upper = 0.9375 + 0.89375 * jnp.cos(wave) - 0.0375 * jnp.cos(2.0 * wave) + 0.00625 * jnp.cos(3.0 * wave)
    return upper / (1.0 + 0.8 * jnp.cos(wave))

def derive_symbol(cells):
    wave = 2.0 * jnp.pi * jnp.arange(cells // 2 + 1, dtype=jnp.float32) / cells
    upper = 14.0 / 9.0 * jnp.sin(wave) + 1.0 / 18.0 * jnp.sin(2.0 * wave)
    return 1j * (upper / (1.0 + 2.0 / 3.0 * jnp.cos(wave)))

def along_axis(field, axis_dim, symbol):
    cells = field.shape[axis_dim]
    shape = [1] * field.ndim
    shape[axis_dim] = cells // 2 + 1
    spectrum = jnp.fft.rfft(field, axis=axis_dim)
    return jnp.fft.irfft(spectrum * symbol.reshape(shape), n=cells, axis=axis_dim)

def plane_step(plane):
    cells_x = plane.shape[1]
    cells_y = plane.shape[2]
    pairs = ((0, 0), (0, 1), (0, 2), (1, 1), (1, 2), (2, 2))
    products = jnp.stack([plane[first] * plane[second] for first, second in pairs])
    fields = jnp.concatenate((plane, products), axis=0)
    filtered = along_axis(along_axis(fields, 1, filter_symbol(cells_x)), 2, filter_symbol(cells_y))
    smooth = filtered[:3]
    leonard = filtered[3:] - jnp.stack([smooth[first] * smooth[second] for first, second in pairs])
    grad_x = along_axis(smooth, 1, derive_symbol(cells_x))
    grad_y = along_axis(smooth, 2, derive_symbol(cells_y))
    sxx = grad_x[0]
    syy = grad_y[1]
    szz = -(sxx + syy)
    sxy = 0.5 * (grad_y[0] + grad_x[1])
    sxz = 0.5 * grad_x[2]
    syz = 0.5 * grad_y[2]
    magnitude = jnp.sqrt(2.0 * (sxx * sxx + syy * syy + szz * szz + 2.0 * (sxy * sxy + sxz * sxz + syz * syz)))
    model = magnitude[None] * jnp.stack((sxx, sxy, sxz, syy, syz, szz))
    pair_weight = jnp.array([1.0, 2.0, 2.0, 1.0, 2.0, 1.0], dtype=jnp.float32).reshape(6, 1, 1)
    count = cells_x * cells_y
    cross = jnp.sum(pair_weight * leonard * model) / count
    square = jnp.sum(pair_weight * model * model) / count
    coefficient = cross / (square + 1e-06)
    along_x = along_axis(jnp.stack((model[0], model[1], model[2])), 1, derive_symbol(cells_x))
    along_y = along_axis(jnp.stack((model[1], model[3], model[4])), 2, derive_symbol(cells_y))
    return (coefficient * (along_x + along_y), coefficient)

def reference(velocity):
    planes = jnp.transpose(velocity, (1, 0, 2, 3))
    divergence, coefficient = lax.map(plane_step, planes)
    return (jnp.transpose(divergence, (1, 0, 2, 3)), coefficient)
```

```python
import jax
import jax.numpy as jnp
import ml_dtypes
import numpy as np
from jax import lax
from jax.experimental import pallas as pl
from jax.experimental.pallas import tpu as pltpu
from jax.sharding import PartitionSpec as P

ROWS = 512
COLS = 256
MARGIN = 32
TILE = 128
WINDOW = TILE + 2 * MARGIN
POLE_F = -0.5
POLE_D = (np.sqrt(5.0) - 3.0) / 2.0
PAIRS = ((0, 0), (0, 1), (0, 2), (1, 1), (1, 2), (2, 2))
NEAR = (3, 3, 3) + (2,) * 9
FAR = (2, 2, 2) + (1,) * 9
SLOTS = tuple(n + f for n, f in zip(NEAR, FAR))
START = tuple(int(s) for s in np.concatenate(([0], np.cumsum(SLOTS)[:-1])))
SENT = sum(SLOTS)
SENT_PAD = 48
DSENT = 2
BF = jnp.bfloat16
F32 = jnp.float32


def kernels(cells=2048):
    wave = 2.0 * np.pi * np.arange(cells // 2 + 1) / cells
    filt = (0.9375 + 0.89375 * np.cos(wave) - 0.0375 * np.cos(2 * wave) + 0.00625 * np.cos(3 * wave)) / (
        1.0 + 0.8 * np.cos(wave)
    )
    deri = 1j * (14.0 / 9.0 * np.sin(wave) + np.sin(2 * wave) / 18.0) / (1.0 + 2.0 / 3.0 * np.cos(wave))
    return tuple(np.fft.irfft(s, n=cells) for s in (filt, deri, deri * filt))


KF, KD, KG = kernels()


def split(table):
    high = np.asarray(table, np.float32).astype(ml_dtypes.bfloat16)
    low = (np.asarray(table, np.float64) - high.astype(np.float64)).astype(ml_dtypes.bfloat16)
    return high, low


def toeplitz(kernel, rows, cols, shift):
    offset = np.arange(rows)[:, None] + shift - np.arange(cols)[None, :]
    return kernel[offset % len(kernel)]


def left_operand(table):
    high, low = split(table)
    return np.concatenate([high, high, low], axis=1)


def right_operand(table):
    high, low = split(table)
    return np.concatenate([high, high, low], axis=0)


def far_fit(kernel, poles, near):
    k = np.arange(near + 1, near + 1 + len(poles))
    weight = np.linalg.solve(np.stack([np.power(p, k) for p in poles], axis=1), kernel[k])
    k = np.arange(1, near + 1)
    rest = kernel[k] - sum(w * np.power(p, k) for w, p in zip(weight, poles))
    return weight, rest


def from_left(kernel, poles, near, slots_near, slots_far):
    weight, rest = far_fit(kernel, poles, near)
    table = np.zeros((slots_near + slots_far, COLS))
    for m in range(1, near + 1):
        for c in range(0, near - m + 1):
            table[m - 1, c] = rest[c + m - 1]
    for s, (w, p) in enumerate(zip(weight, poles)):
        table[slots_near + s] = w * np.power(p, np.arange(COLS, dtype=np.float64))
    return table


def send_table(near, far, poles):
    depth = 64
    table = np.zeros((depth, near + far))
    for m in range(near):
        table[m, m] = 1.0
    for s in range(far):
        table[:, near + s] = np.power(poles[s], np.arange(1, depth + 1, dtype=np.float64))
    return table


def edge_table(near, far, start, width=128, second=64):
    send = send_table(near, far, (POLE_F, POLE_D) if near > 1 else (POLE_D,))
    table = np.zeros((128, width))
    n = near + far
    table[64:, start : start + n] = send[::-1]
    table[:64, second + start : second + start + n] = send
    return table


def x_tables():
    f = toeplitz(KF, TILE, WINDOW, MARGIN)
    g = toeplitz(KG, TILE, WINDOW, MARGIN)
    return left_operand(np.concatenate([f, g], axis=0))


def edge_tables():
    tables = [edge_table(NEAR[i], FAR[i], START[i]) for i in range(12)]
    main, rest = [], []
    for i, table in enumerate(tables):
        high, low = split(table)
        main += [high, high]
        if i < 3:
            rest.append(low)
    return np.concatenate(main + rest, axis=0)


def y_tables():
    f = toeplitz(KF, COLS, COLS, 0).T
    g = toeplitz(KG, COLS, COLS, 0).T
    return right_operand(np.concatenate([f, g], axis=1))


def halo_tables():
    table = np.zeros((2 * SENT, 15 * COLS))
    for out in range(15):
        field = out if out < 12 else out - 12
        if out < 12:
            left = from_left(KF, (POLE_F,), 2, NEAR[field], FAR[field])[:, :]
            if FAR[field] == 2:
                left[NEAR[field] + 1] = 0.0
            sign = 1.0
        else:
            left = from_left(KG, (POLE_F, POLE_D), 3, NEAR[field], FAR[field])
            sign = -1.0
        cols = slice(out * COLS, (out + 1) * COLS)
        table[START[field] : START[field] + SLOTS[field], cols] = left
        table[SENT + START[field] : SENT + START[field] + SLOTS[field], cols] = sign * left[:, ::-1]
    full = np.zeros((256, 15 * COLS), ml_dtypes.bfloat16)
    high, low = split(table)
    n = 2 * SENT
    full[:n], full[n : 2 * n], full[2 * n : 3 * n] = high, high, low
    return full


def d_edge_tables():
    main, rest = [], []
    for i in range(3):
        high, low = split(edge_table(1, 1, 2 * i, second=8))
        main += [high, high]
        rest.append(low)
    return np.concatenate(main + rest, axis=0)


def d_halo_tables():
    table = np.zeros((16, 3 * COLS))
    left = from_left(KD, (POLE_D,), 1, 1, 1)
    for out in range(3):
        cols = slice(out * COLS, (out + 1) * COLS)
        table[2 * out : 2 * out + 2, cols] = left
        table[8 + 2 * out : 8 + 2 * out + 2, cols] = -left[:, ::-1]
    return right_operand(table)


def d_x_tables():
    return left_operand(toeplitz(KD, TILE, WINDOW, MARGIN))


def d_y_tables():
    return right_operand(toeplitz(KD, COLS, COLS, 0).T)


def parts(value):
    high = value.astype(BF)
    return high, (value - high.astype(F32)).astype(BF)


def dot(a, b):
    return jnp.dot(a, b, preferred_element_type=F32)


def x_windows(velocity, windows, table, edge, out, edges_out):
    for t, window in enumerate(windows):
        rows = pl.ds(t * TILE, TILE)
        v = [window(i) for i in range(3)]
        data = v + [v[a] * v[b] for a, b in PAIRS]
        done = [None] * 12
        for i, value in enumerate(data):
            high, low = parts(value)
            stacked = jnp.concatenate([high, low, high], axis=0)
            if i < 3:
                both = dot(table[...], stacked)
                done[i], done[3 + i] = both[:TILE], both[TILE:]
            else:
                done[3 + i] = dot(table[:TILE], stacked)
        lane = lax.broadcasted_iota(jnp.int32, (TILE, 128), 1)
        main, rest = [], []
        for i, value in enumerate(done):
            high, low = parts(value)
            out[i, 0, rows, :] = high
            out[i, 1, rows, :] = low
            mixed = jnp.where(lane < 64, value[:, :128], value[:, 128:])
            high, low = parts(mixed)
            main += [high, low]
            if i < 3:
                rest.append(high)
        sent = dot(jnp.concatenate(main + rest, axis=1), edge[...])
        edges_out(t, sent.T)


def middle_kernel(v, table, edge, out, sent):
    def window(t):
        return lambda i: v[i, pl.ds((t + 1) * TILE - MARGIN, WINDOW), :]

    def put(t, value):
        sent[:, pl.ds(t * TILE, TILE)] = value

    x_windows(v, [window(t) for t in range(ROWS // TILE - 2)], table, edge, out, put)


def outer_kernel(v, before, after, middle, table, edge, out, to_right, to_left):
    def first(i):
        return jnp.concatenate([before[i], v[i, pl.ds(0, TILE + MARGIN), :]], axis=0)

    def last(i):
        return jnp.concatenate([v[i, pl.ds(ROWS - TILE - MARGIN, TILE + MARGIN), :], after[i]], axis=0)

    inner = pl.ds(TILE, ROWS - 2 * TILE)
    to_right[:, inner] = middle[:SENT_PAD]
    to_left[:, inner] = middle[64 : 64 + SENT_PAD]

    def put(t, value):
        place = pl.ds(t * (ROWS - TILE), TILE)
        to_right[:, place] = value[:SENT_PAD]
        to_left[:, place] = value[64 : 64 + SENT_PAD]

    x_windows(v, [first, last], table, edge, out, put)


def y_kernel(middle, outer, table, out):
    def part(source, rows, place):
        for i in range(12):
            high, low = source[i, 0, rows, :], source[i, 1, rows, :]
            data = jnp.concatenate([high, low, high], axis=1)
            if i < 3:
                both = dot(data, table[...])
                out[i, place, :] = both[:, :COLS]
                out[12 + i, place, :] = both[:, COLS:]
            else:
                out[i, place, :] = dot(data, table[:, :COLS])

    part(outer, pl.ds(0, TILE), pl.ds(0, TILE))
    part(middle, pl.ds(0, ROWS - 2 * TILE), pl.ds(TILE, ROWS - 2 * TILE))
    part(outer, pl.ds(TILE, TILE), pl.ds(ROWS - TILE, TILE))


CHUNK = 16


def model_kernel(local, left, right, table, edge, model, first, last, to_right, to_left, sums, halo, added, total):
    high, low = parts(left[...])
    high2, low2 = parts(right[...])
    n = SENT
    halo[...] = jnp.zeros_like(halo)
    for k, (a, b) in enumerate(((high, high2), (low, low2), (high, high2))):
        halo[pl.ds(2 * n * k, n), :] = a.astype(F32)[:n]
        halo[pl.ds(2 * n * k + n, n), :] = b.astype(F32)[:n]
    total[...] = jnp.zeros_like(total)
    for t in range(ROWS // TILE):
        added[...] = dot(halo[:, pl.ds(t * TILE, TILE)].T.astype(BF), table[...])

        def chunk(step, carry):
            near = pl.ds(pl.multiple_of(step * CHUNK, CHUNK), CHUNK)
            rows = pl.ds(pl.multiple_of(t * TILE + step * CHUNK, CHUNK), CHUNK)
            f = [local[i, rows, :] + added[near, pl.ds(i * COLS, COLS)] for i in range(15)]
            smooth, gx, products, gy = f[0:3], f[3:6], f[6:12], f[12:15]
            sxx, syy = gx[0], gy[1]
            szz = -(sxx + syy)
            sxy = 0.5 * (gy[0] + gx[1])
            sxz = 0.5 * gx[2]
            syz = 0.5 * gy[2]
            inner = sxx * sxx + syy * syy + szz * szz + 2.0 * (sxy * sxy + sxz * sxz + syz * syz)
            magnitude = jnp.sqrt(2.0 * inner)
            strain = (sxx, sxy, sxz, syy, syz, szz)
            cross = jnp.zeros((CHUNK, COLS), F32)
            for w, product, (a, b), s in zip((1.0, 2.0, 2.0, 1.0, 2.0, 1.0), products, PAIRS, strain):
                term = (product - smooth[a] * smooth[b]) * s
                cross = cross + (term if w == 1.0 else 2.0 * term)
            for i in range(5):
                model[i, rows, :] = magnitude * strain[i]
            total[0] += cross * magnitude
            total[1] += 2.0 * inner * inner
            return carry

        lax.fori_loop(0, TILE // CHUNK, chunk, 0)
        rows = pl.ds(t * TILE, TILE)
        lane = lax.broadcasted_iota(jnp.int32, (TILE, 128), 1)
        main, rest = [], []
        for i in (1, 3, 4):
            high, low = parts(jnp.where(lane < 64, model[i, rows, pl.ds(0, 128)], model[i, rows, pl.ds(128, 128)]))
            main += [high, low]
            rest.append(high)
        sent = dot(jnp.concatenate(main + rest, axis=1), edge[...]).T
        to_right[:, pl.ds(t * TILE, TILE)] = sent[:8]
        to_left[:, pl.ds(t * TILE, TILE)] = sent[8:16]
    for i in range(3):
        first[i] = model[i, pl.ds(0, MARGIN), :]
        last[i] = model[i, pl.ds(ROWS - MARGIN, MARGIN), :]
    cross, square = jnp.sum(total[0]), jnp.sum(total[1])
    lane = lax.broadcasted_iota(jnp.int32, sums.shape, 1)
    sums[...] = jnp.where(lane < 64, cross, square)


def divergence_kernel(model, before, after, left, right, coefficient, xt, yt, ht, out):
    scale = coefficient[0:1, 0:1]
    halo_l, halo_r = left[...], right[...]
    for t in range(ROWS // TILE):
        rows = pl.ds(t * TILE, TILE)
        halo = jnp.concatenate([halo_l[:, t * TILE : (t + 1) * TILE], halo_r[:, t * TILE : (t + 1) * TILE]], axis=0)
        halo = jnp.concatenate([halo, jnp.zeros((112, TILE), F32)], axis=0).T
        high, low = parts(halo)
        high, low = high[:, :16], low[:, :16]
        added = dot(jnp.concatenate([high, low, high], axis=1), ht[...])
        for c, (i, j) in enumerate(((0, 1), (1, 3), (2, 4))):
            if t == 0:
                window = jnp.concatenate([before[i], model[i, pl.ds(0, TILE + MARGIN), :]], axis=0)
            elif t == ROWS // TILE - 1:
                window = jnp.concatenate([model[i, pl.ds(ROWS - TILE - MARGIN, TILE + MARGIN), :], after[i]], axis=0)
            else:
                window = model[i, pl.ds(t * TILE - MARGIN, WINDOW), :]
            high, low = parts(window)
            along_x = dot(xt[...], jnp.concatenate([high, low, high], axis=0))
            high, low = parts(model[j, rows, :])
            along_y = dot(jnp.concatenate([high, low, high], axis=1), yt[...])
            out[c, rows, :] = scale * (along_x + along_y + added[:, c * COLS : (c + 1) * COLS])


def call(kernel, outs, flops, *args, scratch=()):
    return pl.pallas_call(
        kernel,
        out_shape=[jax.ShapeDtypeStruct(s, d) for s, d in outs],
        in_specs=[pl.BlockSpec(memory_space=pltpu.VMEM)] * len(args),
        out_specs=[pl.BlockSpec(memory_space=pltpu.VMEM)] * len(outs),
        scratch_shapes=list(scratch),
        cost_estimate=pl.CostEstimate(flops=int(flops), bytes_accessed=6 << 20, transcendentals=0),
        compiler_params=pltpu.CompilerParams(vmem_limit_bytes=40 << 20),
    )(*args)


def exchange(to_next, to_previous, axis):
    n = lax.axis_size(axis)
    up = [(i, (i + 1) % n) for i in range(n)]
    down = [(j, i) for i, j in up]
    return lax.ppermute(to_next, axis, up), lax.ppermute(to_previous, axis, down)


def on_device(velocity):
    v = velocity[:, 0]
    before, after = exchange(v[:, ROWS - MARGIN :], v[:, :MARGIN], "gx")
    xt, edge = jnp.asarray(x_tables()), jnp.asarray(edge_tables())
    inner = ROWS - 2 * TILE
    middle, sent = call(
        middle_kernel, [((12, 2, inner, COLS), BF), ((128, inner), F32)], 4e9, v, xt, edge
    )
    outer, to_right, to_left = call(
        outer_kernel,
        [((12, 2, 2 * TILE, COLS), BF), ((SENT_PAD, ROWS), F32), ((SENT_PAD, ROWS), F32)],
        4e9,
        v, before, after, sent, xt, edge,
    )
    left, right = exchange(to_right, to_left, "gy")
    (local,) = call(y_kernel, [((15, ROWS, COLS), F32)], 4e9, middle, outer, jnp.asarray(y_tables()))
    devices = lax.axis_size("gx") * lax.axis_size("gy")
    model, first, last, to_right, to_left, sums = call(
        model_kernel,
        [
            ((5, ROWS, COLS), F32),
            ((3, MARGIN, COLS), F32),
            ((3, MARGIN, COLS), F32),
            ((8, ROWS), F32),
            ((8, ROWS), F32),
            ((devices, 128), F32),
        ],
        4e9,
        local, left, right, jnp.asarray(halo_tables()), jnp.asarray(d_edge_tables()),
        scratch=[
            pltpu.VMEM((256, ROWS), F32),
            pltpu.VMEM((TILE, 15 * COLS), F32),
            pltpu.VMEM((2, CHUNK, COLS), F32),
        ],
    )
    before, after = exchange(last, first, "gx")
    left, right = exchange(to_right, to_left, "gy")
    sums = lax.all_to_all(sums, ("gx", "gy"), 0, 0, tiled=True)
    sums = jnp.sum(sums, axis=0, keepdims=True) / (devices * ROWS * COLS)
    own = sums[:, 0:1] / (sums[:, 64:65] + 1e-06)
    own = jnp.broadcast_to(own, (8, 128))
    groups = lax.axis_size("gz")
    every = [own] + [
        lax.ppermute(own, "gz", [(i, (i + k) % groups) for i in range(groups)]) for k in range(1, groups)
    ]
    (divergence,) = call(
        divergence_kernel,
        [((3, ROWS, COLS), F32)],
        4e9,
        model, before, after, left, right, own,
        jnp.asarray(d_x_tables()), jnp.asarray(d_y_tables()), jnp.asarray(d_halo_tables()),
    )
    at = lax.axis_index("gz")
    coefficient = jnp.zeros((groups,), F32)
    place = jnp.arange(groups)
    for k, value in enumerate(every):
        coefficient = jnp.where(place == lax.rem(at - k + groups, groups), value[0, 0], coefficient)
    return divergence[:, None], coefficient


def solution(mesh):
    return jax.shard_map(
        on_device,
        mesh=mesh,
        in_specs=(P(None, "gz", "gx", "gy"),),
        out_specs=(P(None, "gz", "gx", "gy"), P()),
        check_vma=False,
    )
```

```python
import jax
import jax.numpy as jnp
import ml_dtypes
import numpy as np
from jax import lax
from jax.experimental import pallas as pl
from jax.experimental.pallas import tpu as pltpu
from jax.sharding import PartitionSpec as P

ROWS = 512
COLS = 256
MARGIN = 32
TILE = 128
WINDOW = TILE + 2 * MARGIN
DMARGIN = 24
DWINDOW = TILE + 2 * DMARGIN
POLE_F = -0.5
POLE_D = (np.sqrt(5.0) - 3.0) / 2.0
PAIRS = ((0, 0), (0, 1), (0, 2), (1, 1), (1, 2), (2, 2))
NEAR = (3, 3, 3) + (2,) * 9
FAR = (2, 2, 2) + (1,) * 9
SLOTS = tuple(n + f for n, f in zip(NEAR, FAR))
START = tuple(int(s) for s in np.concatenate(([0], np.cumsum(SLOTS)[:-1])))
SENT = sum(SLOTS)
SENT_PAD = 48
DSENT = 2
BF = jnp.bfloat16
F32 = jnp.float32


def kernels(cells=2048):
    wave = 2.0 * np.pi * np.arange(cells // 2 + 1) / cells
    filt = (0.9375 + 0.89375 * np.cos(wave) - 0.0375 * np.cos(2 * wave) + 0.00625 * np.cos(3 * wave)) / (
        1.0 + 0.8 * np.cos(wave)
    )
    deri = 1j * (14.0 / 9.0 * np.sin(wave) + np.sin(2 * wave) / 18.0) / (1.0 + 2.0 / 3.0 * np.cos(wave))
    return tuple(np.fft.irfft(s, n=cells) for s in (filt, deri, deri * filt))


KF, KD, KG = kernels()


def split(table):
    high = np.asarray(table, np.float32).astype(ml_dtypes.bfloat16)
    low = (np.asarray(table, np.float64) - high.astype(np.float64)).astype(ml_dtypes.bfloat16)
    return high, low


def toeplitz(kernel, rows, cols, shift):
    offset = np.arange(rows)[:, None] + shift - np.arange(cols)[None, :]
    return kernel[offset % len(kernel)]


def left_operand(table):
    high, low = split(table)
    return np.concatenate([high, high, low], axis=1)


def right_operand(table):
    high, low = split(table)
    return np.concatenate([high, low], axis=0)


def thrice(table, cols=slice(None)):
    half = table.shape[0] // 2
    high, low = table[:half, cols], table[half:, cols]
    return jnp.concatenate([high, high, low], axis=0)


def far_fit(kernel, poles, near):
    k = np.arange(near + 1, near + 1 + len(poles))
    weight = np.linalg.solve(np.stack([np.power(p, k) for p in poles], axis=1), kernel[k])
    k = np.arange(1, near + 1)
    rest = kernel[k] - sum(w * np.power(p, k) for w, p in zip(weight, poles))
    return weight, rest


def from_left(kernel, poles, near, slots_near, slots_far):
    weight, rest = far_fit(kernel, poles, near)
    table = np.zeros((slots_near + slots_far, COLS))
    for m in range(1, near + 1):
        for c in range(0, near - m + 1):
            table[m - 1, c] = rest[c + m - 1]
    for s, (w, p) in enumerate(zip(weight, poles)):
        table[slots_near + s] = w * np.power(p, np.arange(COLS, dtype=np.float64))
    return table


def send_table(near, far, poles):
    depth = 64
    table = np.zeros((depth, near + far))
    for m in range(near):
        table[m, m] = 1.0
    for s in range(far):
        table[:, near + s] = np.power(poles[s], np.arange(1, depth + 1, dtype=np.float64))
    return table


def edge_table(near, far, start, width=128, second=64):
    send = send_table(near, far, (POLE_F, POLE_D) if near > 1 else (POLE_D,))
    table = np.zeros((128, width))
    n = near + far
    table[64:, start : start + n] = send[::-1]
    table[:64, second + start : second + start + n] = send
    return table


def x_tables():
    f = toeplitz(KF, TILE, WINDOW, MARGIN)
    g = toeplitz(KG, TILE, WINDOW, MARGIN)
    return left_operand(np.concatenate([f, g], axis=0))


def edge_tables():
    tables = [edge_table(NEAR[i], FAR[i], START[i]) for i in range(12)]
    main, rest = [], []
    for i, table in enumerate(tables):
        high, low = split(table)
        main.append(high)
        if i < 3:
            rest.append(low)
    return np.concatenate(main + rest, axis=0)


def edge_operand(edge, fields, low):
    block = [edge[pl.ds(i * 128, 128), :] for i in range(fields + low)]
    return jnp.concatenate([b for b in block[:fields] for _ in range(2)] + block[fields:], axis=0)


def y_tables():
    f = toeplitz(KF, COLS, COLS, 0).T
    g = toeplitz(KG, COLS, COLS, 0).T
    return right_operand(np.concatenate([f, g], axis=1))


def halo_tables():
    table = np.zeros((2 * SENT, 15 * COLS))
    for out in range(15):
        field = out if out < 12 else out - 12
        if out < 12:
            left = from_left(KF, (POLE_F,), 2, NEAR[field], FAR[field])[:, :]
            if FAR[field] == 2:
                left[NEAR[field] + 1] = 0.0
            sign = 1.0
        else:
            left = from_left(KG, (POLE_F, POLE_D), 3, NEAR[field], FAR[field])
            sign = -1.0
        cols = slice(out * COLS, (out + 1) * COLS)
        table[START[field] : START[field] + SLOTS[field], cols] = left
        table[SENT + START[field] : SENT + START[field] + SLOTS[field], cols] = sign * left[:, ::-1]
    full = np.zeros((256, 15 * COLS), ml_dtypes.bfloat16)
    high, low = split(table)
    n = 2 * SENT
    full[:n], full[n : 2 * n], full[2 * n : 3 * n] = high, high, low
    return full


def d_edge_tables():
    main, rest = [], []
    for i in range(3):
        high, low = split(edge_table(1, 1, 2 * i, second=8))
        main.append(high)
        rest.append(low)
    return np.concatenate(main + rest, axis=0)


def d_halo_tables():
    table = np.zeros((16, 3 * COLS))
    left = from_left(KD, (POLE_D,), 1, 1, 1)
    for out in range(3):
        cols = slice(out * COLS, (out + 1) * COLS)
        table[2 * out : 2 * out + 2, cols] = left
        table[8 + 2 * out : 8 + 2 * out + 2, cols] = -left[:, ::-1]
    return right_operand(table)


def d_x_tables():
    return left_operand(toeplitz(KD, TILE, DWINDOW, DMARGIN))


def d_y_tables():
    return right_operand(toeplitz(KD, COLS, COLS, 0).T)


def parts(value):
    high = value.astype(BF)
    return high, (value - high.astype(F32)).astype(BF)


def dot(a, b):
    return jnp.dot(a, b, preferred_element_type=F32)


def x_windows(velocity, windows, table, edge, out, edges_out):
    for t, window in enumerate(windows):
        rows = pl.ds(t * TILE, TILE)
        v = [window(i) for i in range(3)]
        data = v + [v[a] * v[b] for a, b in PAIRS]
        done = [None] * 12
        for i, value in enumerate(data):
            high, low = parts(value)
            stacked = jnp.concatenate([high, low, high], axis=0)
            if i < 3:
                both = dot(table[...], stacked)
                done[i], done[3 + i] = both[:TILE], both[TILE:]
            else:
                done[3 + i] = dot(table[:TILE], stacked)
        lane = lax.broadcasted_iota(jnp.int32, (TILE, 128), 1)
        main, rest = [], []
        for i, value in enumerate(done):
            high, low = parts(value)
            out[i, 0, rows, :] = high
            out[i, 1, rows, :] = low
            mixed = jnp.where(lane < 64, value[:, :128], value[:, 128:])
            high, low = parts(mixed)
            main += [high, low]
            if i < 3:
                rest.append(high)
        sent = dot(jnp.concatenate(main + rest, axis=1), edge_operand(edge, 12, 3))
        edges_out(t, sent.T)


def strip_kernel(v, first, last):
    first[...] = v[:, pl.ds(0, MARGIN), :]
    last[...] = v[:, pl.ds(ROWS - MARGIN, MARGIN), :]


def middle_kernel(v, table, edge, out, sent):
    def window(t):
        return lambda i: v[i, pl.ds((t + 1) * TILE - MARGIN, WINDOW), :]

    def put(t, value):
        sent[:, pl.ds(t * TILE, TILE)] = value

    x_windows(v, [window(t) for t in range(ROWS // TILE - 2)], table, edge, out, put)


def outer_kernel(v, before, after, middle, table, edge, out, to_right, to_left):
    def first(i):
        return jnp.concatenate([before[i], v[i, pl.ds(0, TILE + MARGIN), :]], axis=0)

    def last(i):
        return jnp.concatenate([v[i, pl.ds(ROWS - TILE - MARGIN, TILE + MARGIN), :], after[i]], axis=0)

    inner = pl.ds(TILE, ROWS - 2 * TILE)
    to_right[:, inner] = middle[:SENT_PAD]
    to_left[:, inner] = middle[64 : 64 + SENT_PAD]

    def put(t, value):
        place = pl.ds(t * (ROWS - TILE), TILE)
        to_right[:, place] = value[:SENT_PAD]
        to_left[:, place] = value[64 : 64 + SENT_PAD]

    x_windows(v, [first, last], table, edge, out, put)


def y_kernel(middle, outer, table, out):
    def part(source, rows, place):
        for i in range(12):
            high, low = source[i, 0, rows, :], source[i, 1, rows, :]
            data = jnp.concatenate([high, low, high], axis=1)
            if i < 3:
                both = dot(data, thrice(table))
                out[i, place, :] = both[:, :COLS]
                out[12 + i, place, :] = both[:, COLS:]
            else:
                out[i, place, :] = dot(data, thrice(table, slice(0, COLS)))

    part(outer, pl.ds(0, TILE), pl.ds(0, TILE))
    part(middle, pl.ds(0, ROWS - 2 * TILE), pl.ds(TILE, ROWS - 2 * TILE))
    part(outer, pl.ds(TILE, TILE), pl.ds(ROWS - TILE, TILE))


CHUNK = 16


def model_kernel(local, left, right, table, edge, model, first, last, to_right, to_left, sums, halo, added, total):
    high, low = parts(left[...])
    high2, low2 = parts(right[...])
    n = SENT
    halo[...] = jnp.zeros_like(halo)
    for k, (a, b) in enumerate(((high, high2), (low, low2), (high, high2))):
        halo[pl.ds(2 * n * k, n), :] = a.astype(F32)[:n]
        halo[pl.ds(2 * n * k + n, n), :] = b.astype(F32)[:n]
    total[...] = jnp.zeros_like(total)
    for t in range(ROWS // TILE):
        added[...] = dot(halo[:, pl.ds(t * TILE, TILE)].T.astype(BF), table[...])

        def chunk(step, carry):
            near = pl.ds(pl.multiple_of(step * CHUNK, CHUNK), CHUNK)
            rows = pl.ds(pl.multiple_of(t * TILE + step * CHUNK, CHUNK), CHUNK)
            f = [local[i, rows, :] + added[near, pl.ds(i * COLS, COLS)] for i in range(15)]
            smooth, gx, products, gy = f[0:3], f[3:6], f[6:12], f[12:15]
            sxx, syy = gx[0], gy[1]
            szz = -(sxx + syy)
            sxy = 0.5 * (gy[0] + gx[1])
            sxz = 0.5 * gx[2]
            syz = 0.5 * gy[2]
            inner = sxx * sxx + syy * syy + szz * szz + 2.0 * (sxy * sxy + sxz * sxz + syz * syz)
            magnitude = jnp.sqrt(2.0 * inner)
            strain = (sxx, sxy, sxz, syy, syz, szz)
            cross = jnp.zeros((CHUNK, COLS), F32)
            for w, product, (a, b), s in zip((1.0, 2.0, 2.0, 1.0, 2.0, 1.0), products, PAIRS, strain):
                term = (product - smooth[a] * smooth[b]) * s
                cross = cross + (term if w == 1.0 else 2.0 * term)
            for i in range(5):
                model[i, rows, :] = magnitude * strain[i]
            total[0] += cross * magnitude
            total[1] += 2.0 * inner * inner
            return carry

        lax.fori_loop(0, TILE // CHUNK, chunk, 0)
        rows = pl.ds(t * TILE, TILE)
        lane = lax.broadcasted_iota(jnp.int32, (TILE, 128), 1)
        main, rest = [], []
        for i in (1, 3, 4):
            high, low = parts(jnp.where(lane < 64, model[i, rows, pl.ds(0, 128)], model[i, rows, pl.ds(128, 128)]))
            main += [high, low]
            rest.append(high)
        sent = dot(jnp.concatenate(main + rest, axis=1), edge_operand(edge, 3, 3)).T
        to_right[:, pl.ds(t * TILE, TILE)] = sent[:8]
        to_left[:, pl.ds(t * TILE, TILE)] = sent[8:16]
    for i in range(3):
        first[i] = model[i, pl.ds(0, DMARGIN), :]
        last[i] = model[i, pl.ds(ROWS - DMARGIN, DMARGIN), :]
    cross, square = jnp.sum(total[0]), jnp.sum(total[1])
    lane = lax.broadcasted_iota(jnp.int32, sums.shape, 1)
    sums[...] = jnp.where(lane < 64, cross, square)


def divergence_kernel(model, before, after, left, right, sums, xt, yt, ht, out, coefficient):
    groups = coefficient.shape[0]
    part = sums[...]
    plane = lax.broadcasted_iota(jnp.int32, part.shape, 0) % groups
    at = lax.axis_index("gz")
    scale = jnp.zeros((1, 1), F32)
    for g in range(groups):
        mean = jnp.sum(jnp.where(plane == g, part, 0.0), axis=0, keepdims=True) * (
            groups / (part.shape[0] * ROWS * COLS)
        )
        value = mean[:, 0:1] / (mean[:, 64:65] + 1e-06)
        coefficient[g] = value[0, 0]
        scale = jnp.where(at == g, value, scale)
    halo_l, halo_r = left[...], right[...]
    for t in range(ROWS // TILE):
        rows = pl.ds(t * TILE, TILE)
        halo = jnp.concatenate([halo_l[:, t * TILE : (t + 1) * TILE], halo_r[:, t * TILE : (t + 1) * TILE]], axis=0)
        halo = jnp.concatenate([halo, jnp.zeros((112, TILE), F32)], axis=0).T
        high, low = parts(halo)
        high, low = high[:, :16], low[:, :16]
        added = dot(jnp.concatenate([high, low, high], axis=1), thrice(ht))
        for c, (i, j) in enumerate(((0, 1), (1, 3), (2, 4))):
            if t == 0:
                window = jnp.concatenate([before[i], model[i, pl.ds(0, TILE + DMARGIN), :]], axis=0)
            elif t == ROWS // TILE - 1:
                window = jnp.concatenate([model[i, pl.ds(ROWS - TILE - DMARGIN, TILE + DMARGIN), :], after[i]], axis=0)
            else:
                window = model[i, pl.ds(t * TILE - DMARGIN, DWINDOW), :]
            high, low = parts(window)
            along_x = dot(xt[...], jnp.concatenate([high, low, high], axis=0))
            high, low = parts(model[j, rows, :])
            along_y = dot(jnp.concatenate([high, low, high], axis=1), thrice(yt))
            out[c, rows, :] = scale * (along_x + along_y + added[:, c * COLS : (c + 1) * COLS])


VMEM = pl.BlockSpec(memory_space=pltpu.VMEM)


def call(kernel, outs, flops, limit, *args, scratch=(), out_specs=None):
    return pl.pallas_call(
        kernel,
        out_shape=[jax.ShapeDtypeStruct(s, d) for s, d in outs],
        in_specs=[VMEM] * len(args),
        out_specs=out_specs or [VMEM] * len(outs),
        scratch_shapes=list(scratch),
        cost_estimate=pl.CostEstimate(flops=int(flops), bytes_accessed=6 << 20, transcendentals=0),
        compiler_params=pltpu.CompilerParams(vmem_limit_bytes=limit << 20),
    )(*args)


def exchange(to_next, to_previous, axis):
    n = lax.axis_size(axis)
    up = [(i, (i + 1) % n) for i in range(n)]
    down = [(j, i) for i, j in up]
    return lax.ppermute(to_next, axis, up), lax.ppermute(to_previous, axis, down)


def on_device(velocity):
    v = velocity[:, 0]
    xt, edge = jnp.asarray(x_tables()), jnp.asarray(edge_tables())
    strip = ((3, MARGIN, COLS), F32)
    first, last = call(strip_kernel, [strip, strip], 2e11, 2, v)
    before, after = exchange(last, first, "gx")
    inner = ROWS - 2 * TILE
    middle, sent = call(
        middle_kernel, [((12, 2, inner, COLS), BF), ((128, inner), F32)], 4e9, 8, v, xt, edge
    )
    outer, to_right, to_left = call(
        outer_kernel,
        [((12, 2, 2 * TILE, COLS), BF), ((SENT_PAD, ROWS), F32), ((SENT_PAD, ROWS), F32)],
        4e9, 8,
        v, before, after, sent, xt, edge,
    )
    left, right = exchange(to_right, to_left, "gy")
    (local,) = call(y_kernel, [((15, ROWS, COLS), F32)], 4e9, 8, middle, outer, jnp.asarray(y_tables()))
    devices = lax.axis_size("gx") * lax.axis_size("gy") * lax.axis_size("gz")
    strip = ((3, DMARGIN, COLS), F32)
    model, first, last, to_right, to_left, sums = call(
        model_kernel,
        [
            ((5, ROWS, COLS), F32),
            strip,
            strip,
            ((8, ROWS), F32),
            ((8, ROWS), F32),
            ((devices, 128), F32),
        ],
        4e9, 12,
        local, left, right, jnp.asarray(halo_tables()), jnp.asarray(d_edge_tables()),
        scratch=[
            pltpu.VMEM((256, ROWS), F32),
            pltpu.VMEM((TILE, 15 * COLS), F32),
            pltpu.VMEM((2, CHUNK, COLS), F32),
        ],
    )
    before, after = exchange(last, first, "gx")
    left, right = exchange(to_right, to_left, "gy")
    sums = lax.all_to_all(sums, ("gx", "gy", "gz"), 0, 0, tiled=True)
    divergence, coefficient = call(
        divergence_kernel,
        [((3, ROWS, COLS), F32), ((lax.axis_size("gz"),), F32)],
        4e9, 8,
        model, before, after, left, right, sums,
        jnp.asarray(d_x_tables()), jnp.asarray(d_y_tables()), jnp.asarray(d_halo_tables()),
        out_specs=[VMEM, pl.BlockSpec(memory_space=pltpu.SMEM)],
    )
    return divergence[:, None], coefficient


def solution(mesh):
    return jax.shard_map(
        on_device,
        mesh=mesh,
        in_specs=(P(None, "gz", "gx", "gy"),),
        out_specs=(P(None, "gz", "gx", "gy"), P()),
        check_vma=False,
    )
```

```python
import jax
import jax.numpy as jnp
import ml_dtypes
import numpy as np
from jax import lax
from jax.experimental import pallas as pl
from jax.experimental.pallas import tpu as pltpu
from jax.sharding import PartitionSpec as P

ROWS = 512
COLS = 256
MARGIN = 32
TILE = 128
WINDOW = TILE + 2 * MARGIN
INNER = ROWS - 2 * MARGIN
REACH = 64
POLE_F = -0.5
POLE_D = (np.sqrt(5.0) - 3.0) / 2.0
PAIRS = ((0, 0), (0, 1), (0, 2), (1, 1), (1, 2), (2, 2))
NEAR = (3, 3, 3) + (2,) * 9
FAR = (2, 2, 2) + (1,) * 9
SLOTS = tuple(n + f for n, f in zip(NEAR, FAR))
START = tuple(int(s) for s in np.concatenate(([0], np.cumsum(SLOTS)[:-1])))
SENT = sum(SLOTS)
SENT_PAD = 48
DSENT = 2
BF = jnp.bfloat16
F32 = jnp.float32


def kernels(cells=2048):
    wave = 2.0 * np.pi * np.arange(cells // 2 + 1) / cells
    filt = (0.9375 + 0.89375 * np.cos(wave) - 0.0375 * np.cos(2 * wave) + 0.00625 * np.cos(3 * wave)) / (
        1.0 + 0.8 * np.cos(wave)
    )
    deri = 1j * (14.0 / 9.0 * np.sin(wave) + np.sin(2 * wave) / 18.0) / (1.0 + 2.0 / 3.0 * np.cos(wave))
    return tuple(np.fft.irfft(s, n=cells) for s in (filt, deri, deri * filt))


KF, KD, KG = kernels()


def split(table):
    high = np.asarray(table, np.float32).astype(ml_dtypes.bfloat16)
    low = (np.asarray(table, np.float64) - high.astype(np.float64)).astype(ml_dtypes.bfloat16)
    return high, low


def toeplitz(kernel, rows, cols, shift):
    offset = np.arange(rows)[:, None] + shift - np.arange(cols)[None, :]
    return kernel[offset % len(kernel)]


def left_operand(table):
    high, low = split(table)
    return np.concatenate([high, high, low], axis=1)


def right_operand(table):
    high, low = split(table)
    return np.concatenate([high, low], axis=0)


def thrice(table, cols=slice(None)):
    half = table.shape[0] // 2
    high, low = table[:half, cols], table[half:, cols]
    return jnp.concatenate([high, high, low], axis=0)


def far_fit(kernel, poles, near):
    k = np.arange(near + 1, near + 1 + len(poles))
    weight = np.linalg.solve(np.stack([np.power(p, k) for p in poles], axis=1), kernel[k])
    k = np.arange(1, near + 1)
    rest = kernel[k] - sum(w * np.power(p, k) for w, p in zip(weight, poles))
    return weight, rest


D_FAR, D_NEAR = [float(x[0]) for x in far_fit(KD, (POLE_D,), 1)]


def from_left(kernel, poles, near, slots_near, slots_far):
    weight, rest = far_fit(kernel, poles, near)
    table = np.zeros((slots_near + slots_far, COLS))
    for m in range(1, near + 1):
        for c in range(0, near - m + 1):
            table[m - 1, c] = rest[c + m - 1]
    for s, (w, p) in enumerate(zip(weight, poles)):
        table[slots_near + s] = w * np.power(p, np.arange(COLS, dtype=np.float64))
    return table


def send_table(near, far, poles):
    depth = 64
    table = np.zeros((depth, near + far))
    for m in range(near):
        table[m, m] = 1.0
    for s in range(far):
        table[:, near + s] = np.power(poles[s], np.arange(1, depth + 1, dtype=np.float64))
    return table


def edge_table(near, far, start, width=128, second=64):
    send = send_table(near, far, (POLE_F, POLE_D) if near > 1 else (POLE_D,))
    table = np.zeros((128, width))
    n = near + far
    table[64:, start : start + n] = send[::-1]
    table[:64, second + start : second + start + n] = send
    return table


def x_tables(tile):
    f = toeplitz(KF, tile, tile + 2 * MARGIN, MARGIN)
    g = toeplitz(KG, tile, tile + 2 * MARGIN, MARGIN)
    return left_operand(np.concatenate([f, g], axis=0))


def edge_tables():
    tables = [edge_table(NEAR[i], FAR[i], START[i]) for i in range(12)]
    main, rest = [], []
    for i, table in enumerate(tables):
        high, low = split(table)
        main.append(high)
        if i < 3:
            rest.append(low)
    return np.concatenate(main + rest, axis=0)


def edge_operand(edge, fields, low):
    block = [edge[pl.ds(i * 128, 128), :] for i in range(fields + low)]
    return jnp.concatenate([b for b in block[:fields] for _ in range(2)] + block[fields:], axis=0)


def y_tables():
    f = toeplitz(KF, COLS, COLS, 0).T
    g = toeplitz(KG, COLS, COLS, 0).T
    return right_operand(np.concatenate([f, g], axis=1))


def halo_tables():
    table = np.zeros((2 * SENT, 15 * 128))
    for out in range(15):
        field = out if out < 12 else out - 12
        if out < 12:
            left = from_left(KF, (POLE_F,), 2, NEAR[field], FAR[field])
            if FAR[field] == 2:
                left[NEAR[field] + 1] = 0.0
            sign = 1.0
        else:
            left = from_left(KG, (POLE_F, POLE_D), 3, NEAR[field], FAR[field])
            sign = -1.0
        left = left[:, :REACH]
        start = START[field]
        table[start : start + SLOTS[field], out * 128 : out * 128 + REACH] = left
        table[SENT + start : SENT + start + SLOTS[field], out * 128 + REACH : (out + 1) * 128] = sign * left[:, ::-1]
    full = np.zeros((256, 15 * 128), ml_dtypes.bfloat16)
    high, low = split(table)
    n = 2 * SENT
    full[:n], full[n : 2 * n], full[2 * n : 3 * n] = high, high, low
    return full


def d_edge_tables():
    main, rest = [], []
    for i in range(3):
        high, low = split(edge_table(1, 1, 2 * i, second=8))
        main.append(high)
        rest.append(low)
    return np.concatenate(main + rest, axis=0)


def d_halo_tables():
    table = np.zeros((16, 3 * 128))
    left = from_left(KD, (POLE_D,), 1, 1, 1)[:, :REACH]
    for out in range(3):
        table[2 * out : 2 * out + 2, out * 128 : out * 128 + REACH] = left
        table[8 + 2 * out : 8 + 2 * out + 2, out * 128 + REACH : (out + 1) * 128] = -left[:, ::-1]
    return right_operand(table)


def d_x_tables():
    return left_operand(toeplitz(KD, TILE, WINDOW, MARGIN))


def d_powers(length, sign=1.0):
    row = lax.broadcasted_iota(jnp.int32, (8, 1), 0)
    column = jnp.zeros((8, 1), F32)
    for s in range(8):
        power = POLE_D ** (s + 1) if sign > 0 else POLE_D ** (8 - s)
        column = jnp.where(row == s, float(power), column)
    blocks = range(length // 8) if sign > 0 else range(length // 8 - 1, -1, -1)
    return jnp.concatenate([column * float(POLE_D ** (8 * k)) for k in blocks], axis=0)


def d_y_tables():
    return right_operand(toeplitz(KD, COLS, COLS, 0).T)


def parts(value):
    high = value.astype(BF)
    return high, (value - high.astype(F32)).astype(BF)


def dot(a, b):
    return jnp.dot(a, b, preferred_element_type=F32)


def x_tile(window, tile, table, edge, put):
    v = [window(i) for i in range(3)]
    data = v + [v[a] * v[b] for a, b in PAIRS]
    done = [None] * 12
    for i, value in enumerate(data):
        high, low = parts(value)
        stacked = jnp.concatenate([high, low, high], axis=0)
        if i < 3:
            both = dot(table[...], stacked)
            done[i], done[3 + i] = both[:tile], both[tile:]
        else:
            done[3 + i] = dot(table[pl.ds(0, tile), :], stacked)
    lane = lax.broadcasted_iota(jnp.int32, (tile, 128), 1)
    main, rest = [], []
    for i, value in enumerate(done):
        high, low = parts(value)
        put(i, high, low)
        high, low = parts(jnp.where(lane < 64, value[:, :128], value[:, 128:]))
        main += [high, low]
        if i < 3:
            rest.append(high)
    return dot(jnp.concatenate(main + rest, axis=1), edge_operand(edge, 12, 3))


def strip_kernel(v, first, last):
    first[...] = v[:, pl.ds(0, MARGIN), :]
    last[...] = v[:, pl.ds(ROWS - MARGIN, MARGIN), :]


def middle_kernel(v, table, small, edge, out, sent):
    at = 0
    while at < INNER:
        tile = min(TILE, INNER - at)
        rows = pl.ds(at, tile)

        def put(i, high, low):
            out[i, 0, rows, :] = high
            out[i, 1, rows, :] = low

        window = lambda i: v[i, pl.ds(at, tile + 2 * MARGIN), :]
        sent[rows, :] = x_tile(window, tile, table if tile == TILE else small, edge, put)
        at += tile


def outer_kernel(v, before, after, middle, table, edge, out, to_right, to_left):
    def first(i):
        return jnp.concatenate([before[i], v[i, pl.ds(0, 2 * MARGIN), :]], axis=0)

    def last(i):
        return jnp.concatenate([v[i, pl.ds(ROWS - 2 * MARGIN, 2 * MARGIN), :], after[i]], axis=0)

    sent = []
    for t, window in enumerate((first, last)):
        rows = pl.ds(t * MARGIN, MARGIN)

        def put(i, high, low):
            out[i, 0, rows, :] = high
            out[i, 1, rows, :] = low

        sent.append(x_tile(window, MARGIN, table, edge, put))
    every = jnp.concatenate([sent[0], middle[...], sent[1]], axis=0).T
    to_right[...] = every[:SENT_PAD]
    to_left[...] = every[64 : 64 + SENT_PAD]


def y_kernel(middle, outer, table, out):
    for i in range(12):
        high, low = [
            jnp.concatenate(
                [outer[i, k, pl.ds(0, MARGIN), :], middle[i, k], outer[i, k, pl.ds(MARGIN, MARGIN), :]], axis=0
            )
            for k in range(2)
        ]
        data = jnp.concatenate([high, low, high], axis=1)
        if i < 3:
            both = dot(data, thrice(table))
            out[i] = both[:, :COLS]
            out[12 + i] = both[:, COLS:]
        else:
            out[i] = dot(data, thrice(table, slice(0, COLS)))


CHUNK = 16


def joined(value, added):
    low = lax.broadcasted_iota(jnp.int32, added.shape, 1) < REACH
    left = value[:, :128] + jnp.where(low, added, 0.0)
    right = value[:, 128:] + jnp.where(low, 0.0, added)
    return jnp.concatenate([left, right], axis=1)


def model_kernel(local, left, right, table, edge, model, first, last, to_right, to_left, sums, halo, added, total):
    high, low = parts(left[...])
    high2, low2 = parts(right[...])
    n = SENT
    halo[...] = jnp.zeros_like(halo)
    for k, (a, b) in enumerate(((high, high2), (low, low2), (high, high2))):
        halo[pl.ds(2 * n * k, n), :] = a.astype(F32)[:n]
        halo[pl.ds(2 * n * k + n, n), :] = b.astype(F32)[:n]
    total[...] = jnp.zeros_like(total)
    for t in range(ROWS // TILE):
        added[...] = dot(halo[:, pl.ds(t * TILE, TILE)].T.astype(BF), table[...])

        def chunk(step, carry):
            near = pl.ds(pl.multiple_of(step * CHUNK, CHUNK), CHUNK)
            rows = pl.ds(pl.multiple_of(t * TILE + step * CHUNK, CHUNK), CHUNK)
            f = [joined(local[i, rows, :], added[near, pl.ds(i * 128, 128)]) for i in range(15)]
            smooth, gx, products, gy = f[0:3], f[3:6], f[6:12], f[12:15]
            sxx, syy = gx[0], gy[1]
            szz = -(sxx + syy)
            sxy = 0.5 * (gy[0] + gx[1])
            sxz = 0.5 * gx[2]
            syz = 0.5 * gy[2]
            inner = sxx * sxx + syy * syy + szz * szz + 2.0 * (sxy * sxy + sxz * sxz + syz * syz)
            magnitude = jnp.sqrt(2.0 * inner)
            strain = (sxx, sxy, sxz, syy, syz, szz)
            cross = jnp.zeros((CHUNK, COLS), F32)
            for w, product, (a, b), s in zip((1.0, 2.0, 2.0, 1.0, 2.0, 1.0), products, PAIRS, strain):
                term = (product - smooth[a] * smooth[b]) * s
                cross = cross + (term if w == 1.0 else 2.0 * term)
            for i in range(5):
                model[i, rows, :] = magnitude * strain[i]
            total[0] += cross * magnitude
            total[1] += 2.0 * inner * inner
            return carry

        lax.fori_loop(0, TILE // CHUNK, chunk, 0)
        rows = pl.ds(t * TILE, TILE)
        lane = lax.broadcasted_iota(jnp.int32, (TILE, 128), 1)
        main, rest = [], []
        for i in (1, 3, 4):
            high, low = parts(jnp.where(lane < 64, model[i, rows, pl.ds(0, 128)], model[i, rows, pl.ds(128, 128)]))
            main += [high, low]
            rest.append(high)
        sent = dot(jnp.concatenate(main + rest, axis=1), edge_operand(edge, 3, 3)).T
        to_right[:, pl.ds(t * TILE, TILE)] = sent[:8]
        to_left[:, pl.ds(t * TILE, TILE)] = sent[8:16]
    near_first, near_last = d_powers(MARGIN), d_powers(MARGIN, -1.0)
    first[...] = jnp.zeros_like(first)
    last[...] = jnp.zeros_like(last)
    for i in range(3):
        first[i : i + 1] = model[i, pl.ds(0, 1), :]
        last[i : i + 1] = model[i, pl.ds(ROWS - 1, 1), :]
        first[i + 3 : i + 4] = jnp.sum(near_first * model[i, pl.ds(0, MARGIN), :], axis=0, keepdims=True)
        last[i + 3 : i + 4] = jnp.sum(near_last * model[i, pl.ds(ROWS - MARGIN, MARGIN), :], axis=0, keepdims=True)
    cross, square = jnp.sum(total[0]), jnp.sum(total[1])
    lane = lax.broadcasted_iota(jnp.int32, sums.shape, 1)
    sums[...] = jnp.where(lane < 64, cross, square)


def local_kernel(model, xt, yt, out, held):
    none = jnp.zeros((MARGIN, COLS), F32)
    for t in range(ROWS // TILE):
        rows = pl.ds(t * TILE, TILE)
        for c, (i, j) in enumerate(((0, 1), (1, 3), (2, 4))):
            if t == 0:
                window = jnp.concatenate([none, model[i, pl.ds(0, TILE + MARGIN), :]], axis=0)
            elif t == ROWS // TILE - 1:
                window = jnp.concatenate([model[i, pl.ds(ROWS - TILE - MARGIN, TILE + MARGIN), :], none], axis=0)
            else:
                window = model[i, pl.ds(t * TILE - MARGIN, WINDOW), :]
            high, low = parts(window)
            along_x = dot(xt[...], jnp.concatenate([high, low, high], axis=0))
            high, low = parts(model[j, rows, :])
            along_y = dot(jnp.concatenate([high, low, high], axis=1), thrice(yt))
            if c == 0:
                held[rows, :] = along_x + along_y
            else:
                out[j, rows, :] = along_x + along_y
    out[0] = held[...]


def divergence_kernel(local, before, after, left, right, sums, ht, out, coefficient, held, sems):
    groups = coefficient.shape[0]
    part = sums[...]
    plane = lax.broadcasted_iota(jnp.int32, part.shape, 0) % groups
    at = lax.axis_index("gz")
    scale = jnp.zeros((1, 1), F32)
    for g in range(groups):
        mean = jnp.sum(jnp.where(plane == g, part, 0.0), axis=0, keepdims=True) * (
            groups / (part.shape[0] * ROWS * COLS)
        )
        value = mean[:, 0:1] / (mean[:, 64:65] + 1e-06)
        coefficient[g] = value[0, 0]
        scale = jnp.where(at == g, value, scale)
    halo = jnp.concatenate([left[...], right[...], jnp.zeros((112, ROWS), F32)], axis=0)
    copies = []
    for t in range(ROWS // TILE):
        rows = pl.ds(t * TILE, TILE)
        high, low = parts(halo[:, t * TILE : (t + 1) * TILE].T)
        high, low = high[:, :16], low[:, :16]
        added = dot(jnp.concatenate([high, low, high], axis=1), thrice(ht))
        for c, i in enumerate((0, 3, 4)):
            held[c, rows, :] = scale * joined(local[i, rows, :], added[:, c * 128 : (c + 1) * 128])
            if t in (0, ROWS // TILE - 1):
                strip, edge, near = (before, 0, 0) if t == 0 else (after, ROWS - MARGIN, ROWS - 1)
                sign = 1.0 if t == 0 else -1.0
                decay = d_powers(MARGIN, sign) * float(sign * D_FAR / POLE_D)
                held[c, pl.ds(edge, MARGIN), :] += scale * (decay * strip[c + 3 : c + 4])
                held[c, pl.ds(near, 1), :] += (sign * D_NEAR) * scale * strip[c : c + 1]
        copy = pltpu.make_async_copy(held.at[:, rows, :], out.at[:, rows, :], sems.at[t])
        copy.start()
        copies.append(copy)
    for copy in copies:
        copy.wait()


VMEM = pl.BlockSpec(memory_space=pltpu.VMEM)


def call(kernel, outs, flops, limit, *args, scratch=(), out_specs=None, aliases=None):
    return pl.pallas_call(
        kernel,
        out_shape=[jax.ShapeDtypeStruct(s, d) for s, d in outs],
        in_specs=[VMEM] * len(args),
        out_specs=out_specs or [VMEM] * len(outs),
        scratch_shapes=list(scratch),
        input_output_aliases=aliases or {},
        cost_estimate=pl.CostEstimate(flops=int(flops), bytes_accessed=6 << 20, transcendentals=0),
        compiler_params=pltpu.CompilerParams(vmem_limit_bytes=limit << 20),
    )(*args)


def exchange(to_next, to_previous, axis):
    n = lax.axis_size(axis)
    up = [(i, (i + 1) % n) for i in range(n)]
    down = [(j, i) for i, j in up]
    return lax.ppermute(to_next, axis, up), lax.ppermute(to_previous, axis, down)


def on_device(velocity):
    v = velocity[:, 0]
    edge = jnp.asarray(edge_tables())
    strip = ((3, MARGIN, COLS), F32)
    first, last = call(strip_kernel, [strip, strip], 2e11, 2, v)
    before, after = exchange(last, first, "gx")
    middle, sent = call(
        middle_kernel,
        [((12, 2, INNER, COLS), BF), ((INNER, 128), F32)],
        4e9, 8,
        v, jnp.asarray(x_tables(TILE)), jnp.asarray(x_tables(INNER % TILE)), edge,
    )
    outer, to_right, to_left = call(
        outer_kernel,
        [((12, 2, 2 * MARGIN, COLS), BF), ((SENT_PAD, ROWS), F32), ((SENT_PAD, ROWS), F32)],
        1e9, 8,
        v, before, after, sent, jnp.asarray(x_tables(MARGIN)), edge,
    )
    left, right = exchange(to_right, to_left, "gy")
    (local,) = call(y_kernel, [((15, ROWS, COLS), F32)], 4e9, 8, middle, outer, jnp.asarray(y_tables()))
    devices = lax.axis_size("gx") * lax.axis_size("gy") * lax.axis_size("gz")
    model, first, last, to_right, to_left, sums = call(
        model_kernel,
        [
            ((5, ROWS, COLS), F32),
            ((8, COLS), F32),
            ((8, COLS), F32),
            ((8, ROWS), F32),
            ((8, ROWS), F32),
            ((devices, 128), F32),
        ],
        4e9, 12,
        local, left, right, jnp.asarray(halo_tables()), jnp.asarray(d_edge_tables()),
        scratch=[
            pltpu.VMEM((256, ROWS), F32),
            pltpu.VMEM((TILE, 15 * 128), F32),
            pltpu.VMEM((2, CHUNK, COLS), F32),
        ],
    )
    sums = lax.all_to_all(sums, ("gx", "gy", "gz"), 0, 0, tiled=True)
    before, after = exchange(last, first, "gx")
    left, right = exchange(to_right, to_left, "gy")
    (local,) = call(
        local_kernel,
        [((5, ROWS, COLS), F32)],
        4e9, 8,
        model, jnp.asarray(d_x_tables()), jnp.asarray(d_y_tables()),
        scratch=[pltpu.VMEM((ROWS, COLS), F32)],
        aliases={0: 0},
    )
    divergence, coefficient = call(
        divergence_kernel,
        [((3, ROWS, COLS), F32), ((lax.axis_size("gz"),), F32)],
        1e9, 8,
        local, before, after, left, right, sums, jnp.asarray(d_halo_tables()),
        out_specs=[pl.BlockSpec(memory_space=pltpu.HBM), pl.BlockSpec(memory_space=pltpu.SMEM)],
        scratch=[pltpu.VMEM((3, ROWS, COLS), F32), pltpu.SemaphoreType.DMA((ROWS // TILE,))],
    )
    return divergence[:, None], coefficient


def solution(mesh):
    return jax.shard_map(
        on_device,
        mesh=mesh,
        in_specs=(P(None, "gz", "gx", "gy"),),
        out_specs=(P(None, "gz", "gx", "gy"), P()),
        check_vma=False,
    )
```

```python
import jax
import jax.numpy as jnp
import ml_dtypes
import numpy as np
from jax import lax
from jax.experimental import pallas as pl
from jax.experimental.pallas import tpu as pltpu
from jax.sharding import PartitionSpec as P

ROWS = 512
COLS = 256
MARGIN = 32
TILE = 128
WINDOW = TILE + 2 * MARGIN
INNER = ROWS - 2 * MARGIN
REACH = 64
POLE_F = -0.5
POLE_D = (np.sqrt(5.0) - 3.0) / 2.0
PAIRS = ((0, 0), (0, 1), (0, 2), (1, 1), (1, 2), (2, 2))
NEAR = (3, 3, 3) + (2,) * 9
FAR = (2, 2, 2) + (1,) * 9
SLOTS = tuple(n + f for n, f in zip(NEAR, FAR))
START = tuple(int(s) for s in np.concatenate(([0], np.cumsum(SLOTS)[:-1])))
SENT = sum(SLOTS)
SENT_PAD = 48
DSENT = 2
BF = jnp.bfloat16
F32 = jnp.float32


def kernels(cells=2048):
    wave = 2.0 * np.pi * np.arange(cells // 2 + 1) / cells
    filt = (0.9375 + 0.89375 * np.cos(wave) - 0.0375 * np.cos(2 * wave) + 0.00625 * np.cos(3 * wave)) / (
        1.0 + 0.8 * np.cos(wave)
    )
    deri = 1j * (14.0 / 9.0 * np.sin(wave) + np.sin(2 * wave) / 18.0) / (1.0 + 2.0 / 3.0 * np.cos(wave))
    return tuple(np.fft.irfft(s, n=cells) for s in (filt, deri, deri * filt))


KF, KD, KG = kernels()


def split(table):
    high = np.asarray(table, np.float32).astype(ml_dtypes.bfloat16)
    low = (np.asarray(table, np.float64) - high.astype(np.float64)).astype(ml_dtypes.bfloat16)
    return high, low


def toeplitz(kernel, rows, cols, shift):
    offset = np.arange(rows)[:, None] + shift - np.arange(cols)[None, :]
    return kernel[offset % len(kernel)]


def left_operand(table):
    high, low = split(table)
    return np.concatenate([high, high, low], axis=1)


def right_operand(table):
    high, low = split(table)
    return np.concatenate([high, low], axis=0)


def thrice(table, cols=slice(None)):
    half = table.shape[0] // 2
    high, low = table[:half, cols], table[half:, cols]
    return jnp.concatenate([high, high, low], axis=0)


def far_fit(kernel, poles, near):
    k = np.arange(near + 1, near + 1 + len(poles))
    weight = np.linalg.solve(np.stack([np.power(p, k) for p in poles], axis=1), kernel[k])
    k = np.arange(1, near + 1)
    rest = kernel[k] - sum(w * np.power(p, k) for w, p in zip(weight, poles))
    return weight, rest


D_FAR, D_NEAR = [float(x[0]) for x in far_fit(KD, (POLE_D,), 1)]


def from_left(kernel, poles, near, slots_near, slots_far):
    weight, rest = far_fit(kernel, poles, near)
    table = np.zeros((slots_near + slots_far, COLS))
    for m in range(1, near + 1):
        for c in range(0, near - m + 1):
            table[m - 1, c] = rest[c + m - 1]
    for s, (w, p) in enumerate(zip(weight, poles)):
        table[slots_near + s] = w * np.power(p, np.arange(COLS, dtype=np.float64))
    return table


def send_table(near, far, poles):
    depth = 64
    table = np.zeros((depth, near + far))
    for m in range(near):
        table[m, m] = 1.0
    for s in range(far):
        table[:, near + s] = np.power(poles[s], np.arange(1, depth + 1, dtype=np.float64))
    return table


def edge_table(near, far, start, width=128, second=64):
    send = send_table(near, far, (POLE_F, POLE_D) if near > 1 else (POLE_D,))
    table = np.zeros((128, width))
    n = near + far
    table[64:, start : start + n] = send[::-1]
    table[:64, second + start : second + start + n] = send
    return table


def x_tables(tile):
    f = toeplitz(KF, tile, tile + 2 * MARGIN, MARGIN)
    g = toeplitz(KG, tile, tile + 2 * MARGIN, MARGIN)
    return left_operand(np.concatenate([f, g], axis=0))


def edge_tables():
    main, rest = [], []
    for i in range(0, 12, 2):
        a, b = [edge_table(NEAR[k], FAR[k], START[k]) for k in (i, i + 1)]
        high, low = split(np.concatenate([a[:32], b[96:], b[:32], a[96:]], axis=0))
        main.append(high)
        if i < 3:
            rest.append(low)
    return np.concatenate(main + rest, axis=0)


def edge_operand(edge, fields, low):
    block = [edge[pl.ds(i * 128, 128), :] for i in range(fields + low)]
    return jnp.concatenate([b for b in block[:fields] for _ in range(2)] + block[fields:], axis=0)


ORDER = np.concatenate([np.arange(64), np.arange(192, 256), np.arange(128, 192), np.arange(64, 128)])


def y_tables():
    f = toeplitz(KF, COLS, COLS, 0).T[:, ORDER]
    g = toeplitz(KG, COLS, COLS, 0).T[:, ORDER]
    return right_operand(np.concatenate([f, g], axis=1))


def halo_tables():
    table = np.zeros((2 * SENT, 15 * 128))
    for out in range(15):
        field = out if out < 12 else out - 12
        if out < 12:
            left = from_left(KF, (POLE_F,), 2, NEAR[field], FAR[field])
            if FAR[field] == 2:
                left[NEAR[field] + 1] = 0.0
            sign = 1.0
        else:
            left = from_left(KG, (POLE_F, POLE_D), 3, NEAR[field], FAR[field])
            sign = -1.0
        left = left[:, :REACH]
        start = START[field]
        table[start : start + SLOTS[field], out * 128 : out * 128 + REACH] = left
        table[SENT + start : SENT + start + SLOTS[field], out * 128 + REACH : (out + 1) * 128] = sign * left[:, ::-1]
    full = np.zeros((256, 15 * 128), ml_dtypes.bfloat16)
    high, low = split(table)
    n = 2 * SENT
    full[:n], full[n : 2 * n], full[2 * n : 3 * n] = high, high, low
    return full


def d_edge_tables():
    main, rest = [], []
    for i in range(3):
        high, low = split(edge_table(1, 1, 2 * i, second=8))
        main.append(high)
        rest.append(low)
    return np.concatenate(main + rest, axis=0)


def d_halo_tables():
    table = np.zeros((16, 3 * 128))
    left = from_left(KD, (POLE_D,), 1, 1, 1)[:, :REACH]
    for out in range(3):
        table[2 * out : 2 * out + 2, out * 128 : out * 128 + REACH] = left
        table[8 + 2 * out : 8 + 2 * out + 2, out * 128 + REACH : (out + 1) * 128] = -left[:, ::-1]
    return right_operand(table)


def d_x_tables():
    return np.concatenate(split(toeplitz(KD, TILE, WINDOW, MARGIN)), axis=0)


def d_powers(length, sign=1.0):
    row = lax.broadcasted_iota(jnp.int32, (8, 1), 0)
    column = jnp.zeros((8, 1), F32)
    for s in range(8):
        power = POLE_D ** (s + 1) if sign > 0 else POLE_D ** (8 - s)
        column = jnp.where(row == s, float(power), column)
    blocks = range(length // 8) if sign > 0 else range(length // 8 - 1, -1, -1)
    return jnp.concatenate([column * float(POLE_D ** (8 * k)) for k in blocks], axis=0)


def d_y_tables():
    return right_operand(toeplitz(KD, COLS, COLS, 0).T[ORDER][:, ORDER])


def parts(value):
    high = value.astype(BF)
    return high, (value - high.astype(F32)).astype(BF)


def dot(a, b):
    return jnp.dot(a, b, preferred_element_type=F32)


def x_tile(window, tile, table, put, mixed, rows):
    v = [window(i) for i in range(3)]
    data = v + [v[a] * v[b] for a, b in PAIRS]
    done = [None] * 12
    for i, value in enumerate(data):
        high, low = parts(value)
        stacked = jnp.concatenate([high, low, high], axis=0)
        if i < 3:
            both = dot(table[...], stacked)
            done[i], done[3 + i] = both[:tile], both[tile:]
        else:
            done[3 + i] = dot(table[pl.ds(0, tile), :], stacked)
    lane = lax.broadcasted_iota(jnp.int32, (tile, 128), 1)
    edges = []
    for i, value in enumerate(done):
        put(i, *parts(value))
        edges.append(jnp.where(lane < 64, value[:, :128], value[:, 128:]))
    for i in range(0, 12, 2):
        both = jnp.where((lane < 32) | (lane >= 96), edges[i], pltpu.roll(edges[i + 1], 64, 1))
        high, low = parts(both)
        mixed[rows, pl.ds(128 * i, 128)] = high
        mixed[rows, pl.ds(128 * i + 128, 128)] = low
        if i < 3:
            mixed[rows, pl.ds(1536 + 64 * i, 128)] = high


def strip_kernel(first, last, first_out, last_out):
    first_out[...], last_out[...] = first[...], last[...]


def middle_kernel(v, table, small, edge, out, sent, mixed):
    at = 0
    while at < INNER:
        tile = min(TILE, INNER - at)
        rows = pl.ds(at, tile)

        def put(i, high, low):
            out[i, 0, rows, :] = high
            out[i, 1, rows, :] = low

        window = lambda i: v[i, pl.ds(at, tile + 2 * MARGIN), :]
        x_tile(window, tile, table if tile == TILE else small, put, mixed, rows)
        at += tile
    sent[...] = dot(mixed[...], edge_operand(edge, 6, 2))


def outer_kernel(v, before, after, middle, table, edge, out, to_right, to_left, mixed):
    def first(i):
        return jnp.concatenate([before[i], v[i, pl.ds(0, 2 * MARGIN), :]], axis=0)

    def last(i):
        return jnp.concatenate([v[i, pl.ds(ROWS - 2 * MARGIN, 2 * MARGIN), :], after[i]], axis=0)

    for t, window in enumerate((first, last)):
        rows = pl.ds(t * MARGIN, MARGIN)

        def put(i, high, low):
            out[i, 0, rows, :] = high
            out[i, 1, rows, :] = low

        x_tile(window, MARGIN, table, put, mixed, rows)
    sent = dot(mixed[...], edge_operand(edge, 6, 2))
    every = jnp.concatenate([sent[:MARGIN], middle[...], sent[MARGIN:]], axis=0).T
    to_right[...] = every[:SENT_PAD]
    to_left[...] = every[64 : 64 + SENT_PAD]


CHUNK = 16


def stress(f, pair_sums):
    smooth, gx, products, gy = f[0:3], f[3:6], f[6:12], f[12:15]
    sxx, syy = gx[0], gy[1]
    szz = -(sxx + syy)
    sxy = 0.5 * (gy[0] + gx[1])
    sxz = 0.5 * gx[2]
    syz = 0.5 * gy[2]
    inner = sxx * sxx + syy * syy + szz * szz + 2.0 * (sxy * sxy + sxz * sxz + syz * syz)
    magnitude = jnp.sqrt(2.0 * inner)
    strain = (sxx, sxy, sxz, syy, syz, szz)
    single, double = [
        sum((products[p] - smooth[PAIRS[p][0]] * smooth[PAIRS[p][1]]) * strain[p] for p in which)
        for which in ((0, 3, 5), (1, 2, 4))
    ]
    pair_sums[0] += (single + 2.0 * double) * magnitude
    pair_sums[1] += 2.0 * inner * inner
    return [magnitude * strain[i] for i in range(5)]


def y_kernel(middle, outer, table, out, model, pair_sums, held):
    for i in range(12):
        high, low = [
            jnp.concatenate(
                [outer[i, k, pl.ds(0, MARGIN), :], middle[i, k], outer[i, k, pl.ds(MARGIN, MARGIN), :]], axis=0
            )
            for k in range(2)
        ]
        data = jnp.concatenate([high, low, high], axis=1)
        done = dot(data, thrice(table) if i < 3 else thrice(table, slice(0, COLS)))
        out[i], held[i] = done[:, :128], done[:, 128:COLS]
        if i < 3:
            out[12 + i], held[12 + i] = done[:, COLS : COLS + 128], done[:, COLS + 128 :]
    pair_sums[...] = jnp.zeros_like(pair_sums)

    def chunk(step, carry):
        rows = pl.ds(pl.multiple_of(step * CHUNK, CHUNK), CHUNK)
        for i, value in enumerate(stress([held[k, rows, :] for k in range(15)], pair_sums)):
            model[i, rows, :] = value
        return carry

    lax.fori_loop(0, ROWS // CHUNK, chunk, 0, unroll=4)


def model_kernel(
    local, inside, inside_sums, left, right, table, edge, model, first, last, to_right, to_left, sums, halo, added, total
):
    high, low = parts(left[...])
    high2, low2 = parts(right[...])
    n = SENT
    halo[...] = jnp.zeros_like(halo)
    for k, (a, b) in enumerate(((high, high2), (low, low2), (high, high2))):
        halo[pl.ds(2 * n * k, n), :] = a.astype(F32)[:n]
        halo[pl.ds(2 * n * k + n, n), :] = b.astype(F32)[:n]
    total[...] = inside_sums[...]
    added[...] = dot(halo[...].T.astype(BF), table[...])

    def chunk(step, carry):
        rows = pl.ds(pl.multiple_of(step * CHUNK, CHUNK), CHUNK)
        f = [local[i, rows, :] + added[rows, pl.ds(i * 128, 128)] for i in range(15)]
        for i, value in enumerate(stress(f, total)):
            model[i, rows, :] = value
        return carry

    lax.fori_loop(0, ROWS // CHUNK, chunk, 0, unroll=4)
    main, rest = [], []
    for i in (1, 3, 4):
        high, low = parts(model[i])
        main += [high, low]
        rest.append(high)
    sent = dot(jnp.concatenate(main + rest, axis=1), edge_operand(edge, 3, 3)).T
    to_right[...] = sent[:8]
    to_left[...] = sent[8:16]
    near_first, near_last = d_powers(MARGIN), d_powers(MARGIN, -1.0)
    first[...] = jnp.zeros_like(first)
    last[...] = jnp.zeros_like(last)
    for k, source in enumerate((model, inside)):
        lanes = pl.ds(128 * k, 128)
        for i in range(3):
            low, high = source[i, pl.ds(0, MARGIN), :], source[i, pl.ds(ROWS - MARGIN, MARGIN), :]
            first[i : i + 1, lanes] = low[:1]
            last[i : i + 1, lanes] = high[MARGIN - 1 :]
            first[i + 3 : i + 4, lanes] = jnp.sum(near_first * low, axis=0, keepdims=True)
            last[i + 3 : i + 4, lanes] = jnp.sum(near_last * high, axis=0, keepdims=True)
    cross, square = jnp.sum(total[0]), jnp.sum(total[1])
    lane = lax.broadcasted_iota(jnp.int32, sums.shape, 1)
    sums[...] = jnp.where(lane < 64, cross, square)


def local_kernel(edge, inside, xt, yt, edge_out, inside_out, held):
    none = jnp.zeros((MARGIN, COLS), F32)

    def model(i, start, length):
        rows = pl.ds(start, length)
        return jnp.concatenate([edge[i, rows, :], inside[i, rows, :]], axis=1)

    for c, (i, j) in enumerate(((0, 1), (1, 3), (2, 4))):
        high, low = parts(model(j, 0, ROWS))
        along_y = dot(jnp.concatenate([high, low, high], axis=1), thrice(yt))
        for start in range(0, ROWS, TILE):
            tile = min(TILE, ROWS - start)
            rows = pl.ds(start, tile)
            begin, end = max(start - MARGIN, 0), min(start + TILE + MARGIN, ROWS)
            window = model(i, begin, end - begin)
            if begin == 0:
                window = jnp.concatenate([none, window], axis=0)
            if window.shape[0] < WINDOW:
                window = jnp.concatenate([window, jnp.zeros((WINDOW - window.shape[0], COLS), F32)], axis=0)
            high, low = parts(window)
            a, b = dot(xt[...], high), dot(xt[pl.ds(0, TILE), :], low)
            both = (a[:tile] + (a[TILE : TILE + tile] + b[:tile])) + along_y[start : start + tile]
            if c == 0:
                held[rows, :] = both
            else:
                edge_out[j, rows, :], inside_out[j, rows, :] = both[:, :128], both[:, 128:]
    edge_out[0], inside_out[0] = held[:, pl.ds(0, 128)], held[:, pl.ds(128, 128)]


def halo_kernel(edge, inside, before, after, left, right, ht, edge_out, inside_out):
    halo = jnp.concatenate([left[...], right[...], jnp.zeros((112, ROWS), F32)], axis=0)
    high, low = parts(halo.T)
    high, low = high[:, :16], low[:, :16]
    added = dot(jnp.concatenate([high, low, high], axis=1), thrice(ht))
    row = lax.broadcasted_iota(jnp.int32, (MARGIN, 1), 0)
    for c, i in enumerate((0, 3, 4)):
        edge_out[i] = edge[i] + added[:, c * 128 : (c + 1) * 128]
        inside_out[i] = inside[i]
        for strip, sign, start in ((before, 1.0, 0), (after, -1.0, ROWS - MARGIN)):
            decay = d_powers(MARGIN, sign) * float(sign * D_FAR / POLE_D)
            near = jnp.where(row == (0 if start == 0 else MARGIN - 1), sign * D_NEAR * strip[c : c + 1], 0.0)
            part = decay * strip[c + 3 : c + 4] + near
            rows = pl.ds(start, MARGIN)
            edge_out[i, rows, :] += part[:, :128]
            inside_out[i, rows, :] += part[:, 128:]


def scale_kernel(edge, inside, sums, out, coefficient, held, sems):
    groups = coefficient.shape[0]
    part = sums[...]
    plane = lax.broadcasted_iota(jnp.int32, part.shape, 0) % groups
    at = lax.axis_index("gz")
    scale = jnp.zeros((1, 1), F32)
    ratios = []
    for g in range(groups):
        mean = jnp.sum(jnp.where(plane == g, part, 0.0), axis=0, keepdims=True) * (
            groups / (part.shape[0] * ROWS * COLS)
        )
        ratios.append(mean[:, 0:1] / (mean[:, 64:65] + 1e-06))
        scale = jnp.where(at == g, ratios[g], scale)
    copies = []
    half = ROWS // 2
    outer = lax.broadcasted_iota(jnp.int32, (half, 128), 1) < 64
    for t in range(2):
        rows = pl.ds(t * half, half)
        for c, i in enumerate((0, 3, 4)):
            e, m = scale * edge[i, rows, :], scale * inside[i, rows, :]
            held[c, rows, pl.ds(0, 128)] = jnp.where(outer, e, m)
            held[c, rows, pl.ds(128, 128)] = jnp.where(outer, m, e)
            copy = pltpu.make_async_copy(held.at[c, rows, :], out.at[c, rows, :], sems.at[t, c])
            copy.start()
            copies.append(copy)
    for g in range(groups):
        coefficient[g] = ratios[g][0, 0]
    for copy in copies:
        copy.wait()


VMEM = pl.BlockSpec(memory_space=pltpu.VMEM)


def call(kernel, outs, flops, limit, *args, scratch=(), out_specs=None, aliases=None):
    return pl.pallas_call(
        kernel,
        out_shape=[jax.ShapeDtypeStruct(s, d) for s, d in outs],
        in_specs=[VMEM] * len(args),
        out_specs=out_specs or [VMEM] * len(outs),
        scratch_shapes=list(scratch),
        input_output_aliases=aliases or {},
        cost_estimate=pl.CostEstimate(flops=int(flops), bytes_accessed=6 << 20, transcendentals=0),
        compiler_params=pltpu.CompilerParams(vmem_limit_bytes=limit << 20),
    )(*args)


def exchange(to_next, to_previous, axis):
    n = lax.axis_size(axis)
    up = [(i, (i + 1) % n) for i in range(n)]
    down = [(j, i) for i, j in up]
    return lax.ppermute(to_next, axis, up), lax.ppermute(to_previous, axis, down)


def on_device(velocity):
    v = velocity[:, 0]
    edge = jnp.asarray(edge_tables())
    strip = ((3, MARGIN, COLS), F32)
    first, last = call(strip_kernel, [strip, strip], 2e11, 2, v[:, :MARGIN], v[:, ROWS - MARGIN :])
    before, after = exchange(last, first, "gx")
    middle, sent = call(
        middle_kernel,
        [((12, 2, INNER, COLS), BF), ((INNER, 128), F32)],
        4e9, 10,
        v, jnp.asarray(x_tables(TILE)), jnp.asarray(x_tables(INNER % TILE)), edge,
        scratch=[pltpu.VMEM((INNER, 1792), BF)],
    )
    outer, to_right, to_left = call(
        outer_kernel,
        [((12, 2, 2 * MARGIN, COLS), BF), ((SENT_PAD, ROWS), F32), ((SENT_PAD, ROWS), F32)],
        1e9, 8,
        v, before, after, sent, jnp.asarray(x_tables(MARGIN)), edge,
        scratch=[pltpu.VMEM((2 * MARGIN, 1792), BF)],
    )
    left, right = exchange(to_right, to_left, "gy")
    half = ((5, ROWS, 128), F32)
    local, inside, inside_sums = call(
        y_kernel,
        [((15, ROWS, 128), F32), half, ((2, CHUNK, 128), F32)],
        4e9, 12,
        middle, outer, jnp.asarray(y_tables()),
        scratch=[pltpu.VMEM((15, ROWS, 128), F32)],
    )
    devices = lax.axis_size("gx") * lax.axis_size("gy") * lax.axis_size("gz")
    model, first, last, to_right, to_left, sums = call(
        model_kernel,
        [
            half,
            ((8, COLS), F32),
            ((8, COLS), F32),
            ((8, ROWS), F32),
            ((8, ROWS), F32),
            ((devices, 128), F32),
        ],
        4e9, 12,
        local, inside, inside_sums, left, right, jnp.asarray(halo_tables()), jnp.asarray(d_edge_tables()),
        scratch=[
            pltpu.VMEM((256, ROWS), F32),
            pltpu.VMEM((ROWS, 15 * 128), F32),
            pltpu.VMEM((2, CHUNK, 128), F32),
        ],
    )
    sums = lax.all_to_all(sums, ("gx", "gy", "gz"), 0, 0, tiled=True)
    before, after = exchange(last, first, "gx")
    left, right = exchange(to_right, to_left, "gy")
    model, inside = call(
        local_kernel,
        [half, half],
        4e9, 8,
        model, inside, jnp.asarray(d_x_tables()), jnp.asarray(d_y_tables()),
        scratch=[pltpu.VMEM((ROWS, COLS), F32)],
        aliases={0: 0, 1: 1},
    )
    field = ((3, ROWS, COLS), F32)
    model, inside = call(
        halo_kernel,
        [half, half],
        1e9, 8,
        model, inside, before, after, left, right, jnp.asarray(d_halo_tables()),
        aliases={0: 0, 1: 1},
    )
    divergence, coefficient = call(
        scale_kernel,
        [field, ((lax.axis_size("gz"),), F32)],
        1e8, 8,
        model, inside, sums,
        out_specs=[pl.BlockSpec(memory_space=pltpu.HBM), pl.BlockSpec(memory_space=pltpu.SMEM)],
        scratch=[pltpu.VMEM((3, ROWS, COLS), F32), pltpu.SemaphoreType.DMA((2, 3))],
    )
    return divergence[:, None], coefficient


def solution(mesh):
    return jax.shard_map(
        on_device,
        mesh=mesh,
        in_specs=(P(None, "gz", "gx", "gy"),),
        out_specs=(P(None, "gz", "gx", "gy"), P()),
        check_vma=False,
    )
```

```python
import jax
import jax.numpy as jnp
import ml_dtypes
import numpy as np
from jax import lax
from jax.experimental import pallas as pl
from jax.experimental.pallas import tpu as pltpu
from jax.sharding import PartitionSpec as P

ROWS = 512
COLS = 256
MARGIN = 32
HALO = 24
TILE = 128
WINDOW = TILE + 2 * MARGIN
INNER = ROWS - 2 * MARGIN
REACH = 64
POLE_F = -0.5
POLE_D = (np.sqrt(5.0) - 3.0) / 2.0
PAIRS = ((0, 0), (0, 1), (0, 2), (1, 1), (1, 2), (2, 2))
NEAR = (3, 3, 3) + (2,) * 9
FAR = (2, 2, 2) + (1,) * 9
SLOTS = tuple(n + f for n, f in zip(NEAR, FAR))
START = tuple(int(s) for s in np.concatenate(([0], np.cumsum(SLOTS)[:-1])))
SENT = sum(SLOTS)
SENT_PAD = 48
DSENT = 2
BF = jnp.bfloat16
F32 = jnp.float32


def kernels(cells=2048):
    wave = 2.0 * np.pi * np.arange(cells // 2 + 1) / cells
    filt = (0.9375 + 0.89375 * np.cos(wave) - 0.0375 * np.cos(2 * wave) + 0.00625 * np.cos(3 * wave)) / (
        1.0 + 0.8 * np.cos(wave)
    )
    deri = 1j * (14.0 / 9.0 * np.sin(wave) + np.sin(2 * wave) / 18.0) / (1.0 + 2.0 / 3.0 * np.cos(wave))
    return tuple(np.fft.irfft(s, n=cells) for s in (filt, deri, deri * filt))


KF, KD, KG = kernels()


def split(table):
    high = np.asarray(table, np.float32).astype(ml_dtypes.bfloat16)
    low = (np.asarray(table, np.float64) - high.astype(np.float64)).astype(ml_dtypes.bfloat16)
    return high, low


def toeplitz(kernel, rows, cols, shift):
    offset = np.arange(rows)[:, None] + shift - np.arange(cols)[None, :]
    return kernel[offset % len(kernel)]


def left_operand(table):
    high, low = split(table)
    return np.concatenate([high, high, low], axis=1)


def right_operand(table):
    high, low = split(table)
    return np.concatenate([high, low], axis=0)


def thrice(table, cols=slice(None)):
    half = table.shape[0] // 2
    high, low = table[:half, cols], table[half:, cols]
    return jnp.concatenate([high, high, low], axis=0)


def far_fit(kernel, poles, near):
    k = np.arange(near + 1, near + 1 + len(poles))
    weight = np.linalg.solve(np.stack([np.power(p, k) for p in poles], axis=1), kernel[k])
    k = np.arange(1, near + 1)
    rest = kernel[k] - sum(w * np.power(p, k) for w, p in zip(weight, poles))
    return weight, rest


D_FAR, D_NEAR = [float(x[0]) for x in far_fit(KD, (POLE_D,), 1)]


def from_left(kernel, poles, near, slots_near, slots_far):
    weight, rest = far_fit(kernel, poles, near)
    table = np.zeros((slots_near + slots_far, COLS))
    for m in range(1, near + 1):
        for c in range(0, near - m + 1):
            table[m - 1, c] = rest[c + m - 1]
    for s, (w, p) in enumerate(zip(weight, poles)):
        table[slots_near + s] = w * np.power(p, np.arange(COLS, dtype=np.float64))
    return table


def send_table(near, far, poles):
    depth = 64
    table = np.zeros((depth, near + far))
    for m in range(near):
        table[m, m] = 1.0
    for s in range(far):
        table[:, near + s] = np.power(poles[s], np.arange(1, depth + 1, dtype=np.float64))
    return table


def edge_table(near, far, start, width=128, second=64):
    send = send_table(near, far, (POLE_F, POLE_D) if near > 1 else (POLE_D,))
    table = np.zeros((128, width))
    n = near + far
    table[64:, start : start + n] = send[::-1]
    table[:64, second + start : second + start + n] = send
    return table


def x_tables(tile):
    f = toeplitz(KF, tile, tile + 2 * MARGIN, MARGIN)
    g = toeplitz(KG, tile, tile + 2 * MARGIN, MARGIN)
    return left_operand(np.concatenate([f, g], axis=0))


def edge_tables():
    main, rest = [], []
    for i in range(0, 12, 2):
        a, b = [edge_table(NEAR[k], FAR[k], START[k]) for k in (i, i + 1)]
        high, low = split(np.concatenate([a[:32], b[96:], b[:32], a[96:]], axis=0))
        main.append(high)
        if i < 3:
            rest.append(low)
    return np.concatenate(main + rest, axis=0)


def edge_operand(edge, fields, low):
    block = [edge[pl.ds(i * 128, 128), :] for i in range(fields + low)]
    return jnp.concatenate([b for b in block[:fields] for _ in range(2)] + block[fields:], axis=0)


ORDER = np.concatenate([np.arange(64), np.arange(192, 256), np.arange(128, 192), np.arange(64, 128)])


def y_tables():
    f = toeplitz(KF, COLS, COLS, 0).T[:, ORDER]
    g = toeplitz(KG, COLS, COLS, 0).T[:, ORDER]
    return right_operand(np.concatenate([f, g], axis=1))


def halo_tables():
    table = np.zeros((2 * SENT, 15 * 128))
    for out in range(15):
        field = out if out < 12 else out - 12
        if out < 12:
            left = from_left(KF, (POLE_F,), 2, NEAR[field], FAR[field])
            if FAR[field] == 2:
                left[NEAR[field] + 1] = 0.0
            sign = 1.0
        else:
            left = from_left(KG, (POLE_F, POLE_D), 3, NEAR[field], FAR[field])
            sign = -1.0
        left = left[:, :REACH]
        start = START[field]
        table[start : start + SLOTS[field], out * 128 : out * 128 + REACH] = left
        table[SENT + start : SENT + start + SLOTS[field], out * 128 + REACH : (out + 1) * 128] = sign * left[:, ::-1]
    full = np.zeros((256, 15 * 128), ml_dtypes.bfloat16)
    high, low = split(table)
    n = 2 * SENT
    full[:n], full[n : 2 * n], full[2 * n : 3 * n] = high, high, low
    return full


def d_edge_tables():
    main, rest = [], []
    for i in range(3):
        high, low = split(edge_table(1, 1, 2 * i, second=8))
        main.append(high)
        rest.append(low)
    return np.concatenate(main + rest, axis=0)


def d_halo_tables():
    table = np.zeros((16, 3 * 128))
    left = from_left(KD, (POLE_D,), 1, 1, 1)[:, :REACH]
    for out in range(3):
        table[2 * out : 2 * out + 2, out * 128 : out * 128 + REACH] = left
        table[8 + 2 * out : 8 + 2 * out + 2, out * 128 + REACH : (out + 1) * 128] = -left[:, ::-1]
    return right_operand(table)


def d_x_tables():
    return np.concatenate(split(toeplitz(KD, TILE, WINDOW, MARGIN)), axis=0)


def d_powers(length, sign=1.0):
    row = lax.broadcasted_iota(jnp.int32, (8, 1), 0)
    column = jnp.zeros((8, 1), F32)
    for s in range(8):
        power = POLE_D ** (s + 1) if sign > 0 else POLE_D ** (8 - s)
        column = jnp.where(row == s, float(power), column)
    blocks = range(length // 8) if sign > 0 else range(length // 8 - 1, -1, -1)
    return jnp.concatenate([column * float(POLE_D ** (8 * k)) for k in blocks], axis=0)


def d_y_tables():
    return right_operand(toeplitz(KD, COLS, COLS, 0).T[ORDER][:, ORDER])


def parts(value):
    high = value.astype(BF)
    return high, (value - high.astype(F32)).astype(BF)


def dot(a, b):
    return jnp.dot(a, b, preferred_element_type=F32)


def x_tile(window, tile, table, put, mixed, rows):
    v = [window(i) for i in range(3)]
    data = v + [v[a] * v[b] for a, b in PAIRS]
    done = [None] * 12
    for i, value in enumerate(data):
        high, low = parts(value)
        stacked = jnp.concatenate([high, low, high], axis=0)
        if i < 3:
            both = dot(table[...], stacked)
            done[i], done[3 + i] = both[:tile], both[tile:]
        else:
            done[3 + i] = dot(table[pl.ds(0, tile), :], stacked)
    lane = lax.broadcasted_iota(jnp.int32, (tile, 128), 1)
    edges = []
    for i, value in enumerate(done):
        put(i, *parts(value))
        edges.append(jnp.where(lane < 64, value[:, :128], value[:, 128:]))
    for i in range(0, 12, 2):
        both = jnp.where((lane < 32) | (lane >= 96), edges[i], pltpu.roll(edges[i + 1], 64, 1))
        high, low = parts(both)
        mixed[rows, pl.ds(128 * i, 128)] = high
        mixed[rows, pl.ds(128 * i + 128, 128)] = low
        if i < 3:
            mixed[rows, pl.ds(1536 + 64 * i, 128)] = high


def strip_kernel(first, last, first_out, last_out):
    first_out[...], last_out[...] = first[...], last[...]


def middle_kernel(v, table, small, edge, out, sent, mixed):
    at = 0
    while at < INNER:
        tile = min(TILE, INNER - at)
        rows = pl.ds(at, tile)

        def put(i, high, low):
            out[i, 0, rows, :] = high
            out[i, 1, rows, :] = low

        window = lambda i: v[i, pl.ds(at, tile + 2 * MARGIN), :]
        x_tile(window, tile, table if tile == TILE else small, put, mixed, rows)
        at += tile
    sent[...] = dot(mixed[...], edge_operand(edge, 6, 2))


def outer_kernel(v, before, after, middle, table, edge, out, to_right, to_left, mixed):
    none = jnp.zeros((MARGIN - HALO, COLS), F32)

    def first(i):
        return jnp.concatenate([none, before[i], v[i, pl.ds(0, 2 * MARGIN), :]], axis=0)

    def last(i):
        return jnp.concatenate([v[i, pl.ds(ROWS - 2 * MARGIN, 2 * MARGIN), :], after[i], none], axis=0)

    for t, window in enumerate((first, last)):
        rows = pl.ds(t * MARGIN, MARGIN)

        def put(i, high, low):
            out[i, 0, rows, :] = high
            out[i, 1, rows, :] = low

        x_tile(window, MARGIN, table, put, mixed, rows)
    sent = dot(mixed[...], edge_operand(edge, 6, 2))
    every = jnp.concatenate([sent[:MARGIN], middle[...], sent[MARGIN:]], axis=0).T
    to_right[...] = every[:SENT_PAD]
    to_left[...] = every[64 : 64 + SENT_PAD]


CHUNK = 16


def stress(f, pair_sums):
    smooth, gx, products, gy = f[0:3], f[3:6], f[6:12], f[12:15]
    sxx, syy = gx[0], gy[1]
    szz = -(sxx + syy)
    sxy = 0.5 * (gy[0] + gx[1])
    sxz = 0.5 * gx[2]
    syz = 0.5 * gy[2]
    inner = sxx * sxx + syy * syy + szz * szz + 2.0 * (sxy * sxy + sxz * sxz + syz * syz)
    magnitude = jnp.sqrt(2.0 * inner)
    strain = (sxx, sxy, sxz, syy, syz, szz)
    single, double = [
        sum((products[p] - smooth[PAIRS[p][0]] * smooth[PAIRS[p][1]]) * strain[p] for p in which)
        for which in ((0, 3, 5), (1, 2, 4))
    ]
    pair_sums[0] += (single + 2.0 * double) * magnitude
    pair_sums[1] += 2.0 * inner * inner
    return [magnitude * strain[i] for i in range(5)]


def y_kernel(middle, outer, table, out, model, pair_sums, held):
    for i in range(12):
        high, low = [
            jnp.concatenate(
                [outer[i, k, pl.ds(0, MARGIN), :], middle[i, k], outer[i, k, pl.ds(MARGIN, MARGIN), :]], axis=0
            )
            for k in range(2)
        ]
        data = jnp.concatenate([high, low, high], axis=1)
        done = dot(data, thrice(table) if i < 3 else thrice(table, slice(0, COLS)))
        out[i], held[i] = done[:, :128], done[:, 128:COLS]
        if i < 3:
            out[12 + i], held[12 + i] = done[:, COLS : COLS + 128], done[:, COLS + 128 :]
    pair_sums[...] = jnp.zeros_like(pair_sums)

    def chunk(step, carry):
        rows = pl.ds(pl.multiple_of(step * CHUNK, CHUNK), CHUNK)
        for i, value in enumerate(stress([held[k, rows, :] for k in range(15)], pair_sums)):
            model[i, rows, :] = value
        return carry

    lax.fori_loop(0, ROWS // CHUNK, chunk, 0, unroll=4)


def model_kernel(
    local, inside_sums, left, right, table, model, sums, halo, added, total
):
    high, low = parts(left[...])
    high2, low2 = parts(right[...])
    n = SENT
    halo[...] = jnp.zeros_like(halo)
    for k, (a, b) in enumerate(((high, high2), (low, low2), (high, high2))):
        halo[pl.ds(2 * n * k, n), :] = a.astype(F32)[:n]
        halo[pl.ds(2 * n * k + n, n), :] = b.astype(F32)[:n]
    total[...] = inside_sums[...]
    added[...] = dot(halo[...].T.astype(BF), table[...])

    def chunk(step, carry):
        rows = pl.ds(pl.multiple_of(step * CHUNK, CHUNK), CHUNK)
        f = [local[i, rows, :] + added[rows, pl.ds(i * 128, 128)] for i in range(15)]
        for i, value in enumerate(stress(f, total)):
            model[i, rows, :] = value
        return carry

    lax.fori_loop(0, ROWS // CHUNK, chunk, 0, unroll=4)
    cross, square = jnp.sum(total[0]), jnp.sum(total[1])
    lane = lax.broadcasted_iota(jnp.int32, sums.shape, 1)
    sums[...] = jnp.where(lane < 64, cross, square)


def send_kernel(model, inside, edge, first, last, to_right, to_left):
    main, rest = [], []
    for i in (1, 3, 4):
        high, low = parts(model[i])
        main += [high, low]
        rest.append(high)
    sent = dot(jnp.concatenate(main + rest, axis=1), edge_operand(edge, 3, 3)).T
    to_right[...] = sent[:8]
    to_left[...] = sent[8:16]
    near_first, near_last = d_powers(MARGIN), d_powers(MARGIN, -1.0)
    first[...] = jnp.zeros_like(first)
    last[...] = jnp.zeros_like(last)
    for k, source in enumerate((model, inside)):
        lanes = pl.ds(128 * k, 128)
        for i in range(3):
            low, high = source[i, pl.ds(0, MARGIN), :], source[i, pl.ds(ROWS - MARGIN, MARGIN), :]
            first[i : i + 1, lanes] = low[:1]
            last[i : i + 1, lanes] = high[MARGIN - 1 :]
            first[i + 3 : i + 4, lanes] = jnp.sum(near_first * low, axis=0, keepdims=True)
            last[i + 3 : i + 4, lanes] = jnp.sum(near_last * high, axis=0, keepdims=True)


def local_kernel(edge, inside, xt, yt, edge_out, inside_out, held):
    none = jnp.zeros((MARGIN, COLS), F32)

    def model(i, start, length):
        rows = pl.ds(start, length)
        return jnp.concatenate([edge[i, rows, :], inside[i, rows, :]], axis=1)

    for c, (i, j) in enumerate(((0, 1), (1, 3), (2, 4))):
        high, low = parts(model(j, 0, ROWS))
        along_y = dot(jnp.concatenate([high, low, high], axis=1), thrice(yt))
        for start in range(0, ROWS, TILE):
            tile = min(TILE, ROWS - start)
            rows = pl.ds(start, tile)
            begin, end = max(start - MARGIN, 0), min(start + TILE + MARGIN, ROWS)
            window = model(i, begin, end - begin)
            if begin == 0:
                window = jnp.concatenate([none, window], axis=0)
            if window.shape[0] < WINDOW:
                window = jnp.concatenate([window, jnp.zeros((WINDOW - window.shape[0], COLS), F32)], axis=0)
            high, low = parts(window)
            a, b = dot(xt[...], high), dot(xt[pl.ds(0, TILE), :], low)
            both = (a[:tile] + (a[TILE : TILE + tile] + b[:tile])) + along_y[start : start + tile]
            if c == 0:
                held[rows, :] = both
            else:
                edge_out[j, rows, :], inside_out[j, rows, :] = both[:, :128], both[:, 128:]
    edge_out[0], inside_out[0] = held[:, pl.ds(0, 128)], held[:, pl.ds(128, 128)]


def halo_kernel(edge, inside, before, after, left, right, ht, edge_out, inside_out):
    halo = jnp.concatenate([left[...], right[...], jnp.zeros((112, ROWS), F32)], axis=0)
    high, low = parts(halo.T)
    high, low = high[:, :16], low[:, :16]
    added = dot(jnp.concatenate([high, low, high], axis=1), thrice(ht))
    row = lax.broadcasted_iota(jnp.int32, (MARGIN, 1), 0)
    for c, i in enumerate((0, 3, 4)):
        edge_out[i] = edge[i] + added[:, c * 128 : (c + 1) * 128]
        inside_out[i] = inside[i]
        for strip, sign, start in ((before, 1.0, 0), (after, -1.0, ROWS - MARGIN)):
            decay = d_powers(MARGIN, sign) * float(sign * D_FAR / POLE_D)
            near = jnp.where(row == (0 if start == 0 else MARGIN - 1), sign * D_NEAR * strip[c : c + 1], 0.0)
            part = decay * strip[c + 3 : c + 4] + near
            rows = pl.ds(start, MARGIN)
            edge_out[i, rows, :] += part[:, :128]
            inside_out[i, rows, :] += part[:, 128:]


def scale_kernel(edge, inside, sums, out, coefficient):
    groups = coefficient.shape[0]
    part = sums[...]
    plane = lax.broadcasted_iota(jnp.int32, part.shape, 0) % groups
    at = lax.axis_index("gz")
    scale = jnp.zeros((1, 1), F32)
    ratios = []
    for g in range(groups):
        mean = jnp.sum(jnp.where(plane == g, part, 0.0), axis=0, keepdims=True) * (
            groups / (part.shape[0] * ROWS * COLS)
        )
        ratios.append(mean[:, 0:1] / (mean[:, 64:65] + 1e-06))
        scale = jnp.where(at == g, ratios[g], scale)
    outer = lax.broadcasted_iota(jnp.int32, (ROWS, 128), 1) < 64
    for c, i in enumerate((0, 3, 4)):
        e, m = scale * edge[i], scale * inside[i]
        out[c, :, pl.ds(0, 128)] = jnp.where(outer, e, m)
        out[c, :, pl.ds(128, 128)] = jnp.where(outer, m, e)
    for g in range(groups):
        coefficient[g] = ratios[g][0, 0]


VMEM = pl.BlockSpec(memory_space=pltpu.VMEM)


def call(kernel, outs, flops, limit, *args, scratch=(), out_specs=None, aliases=None):
    return pl.pallas_call(
        kernel,
        out_shape=[jax.ShapeDtypeStruct(s, d) for s, d in outs],
        in_specs=[VMEM] * len(args),
        out_specs=out_specs or [VMEM] * len(outs),
        scratch_shapes=list(scratch),
        input_output_aliases=aliases or {},
        cost_estimate=pl.CostEstimate(flops=int(flops), bytes_accessed=6 << 20, transcendentals=0),
        compiler_params=pltpu.CompilerParams(vmem_limit_bytes=limit << 20),
    )(*args)


def exchange(to_next, to_previous, axis):
    n = lax.axis_size(axis)
    up = [(i, (i + 1) % n) for i in range(n)]
    down = [(j, i) for i, j in up]
    return lax.ppermute(to_next, axis, up), lax.ppermute(to_previous, axis, down)


def on_device(velocity):
    v = velocity[:, 0]
    edge = jnp.asarray(edge_tables())
    strip = ((3, HALO, COLS), F32)
    first, last = call(strip_kernel, [strip, strip], 2e11, 2, v[:, :HALO], v[:, ROWS - HALO :])
    before, after = exchange(last, first, "gx")
    middle, sent = call(
        middle_kernel,
        [((12, 2, INNER, COLS), BF), ((INNER, 128), F32)],
        4e9, 10,
        v, jnp.asarray(x_tables(TILE)), jnp.asarray(x_tables(INNER % TILE)), edge,
        scratch=[pltpu.VMEM((INNER, 1792), BF)],
    )
    outer, to_right, to_left = call(
        outer_kernel,
        [((12, 2, 2 * MARGIN, COLS), BF), ((SENT_PAD, ROWS), F32), ((SENT_PAD, ROWS), F32)],
        1e9, 8,
        v, before, after, sent, jnp.asarray(x_tables(MARGIN)), edge,
        scratch=[pltpu.VMEM((2 * MARGIN, 1792), BF)],
    )
    left, right = exchange(to_right, to_left, "gy")
    half = ((5, ROWS, 128), F32)
    local, inside, inside_sums = call(
        y_kernel,
        [((15, ROWS, 128), F32), half, ((2, CHUNK, 128), F32)],
        4e9, 12,
        middle, outer, jnp.asarray(y_tables()),
        scratch=[pltpu.VMEM((15, ROWS, 128), F32)],
    )
    devices = lax.axis_size("gx") * lax.axis_size("gy") * lax.axis_size("gz")
    model, sums = call(
        model_kernel,
        [half, ((devices, 128), F32)],
        4e9, 12,
        local, inside_sums, left, right, jnp.asarray(halo_tables()),
        scratch=[
            pltpu.VMEM((256, ROWS), F32),
            pltpu.VMEM((ROWS, 15 * 128), F32),
            pltpu.VMEM((2, CHUNK, 128), F32),
        ],
    )
    sums = lax.all_to_all(sums, ("gx", "gy", "gz"), 0, 0, tiled=True)
    first, last, to_right, to_left = call(
        send_kernel,
        [((8, COLS), F32), ((8, COLS), F32), ((8, ROWS), F32), ((8, ROWS), F32)],
        1e8, 4,
        model, inside, jnp.asarray(d_edge_tables()),
    )
    before, after = exchange(last, first, "gx")
    left, right = exchange(to_right, to_left, "gy")
    model, inside = call(
        local_kernel,
        [half, half],
        4e9, 8,
        model, inside, jnp.asarray(d_x_tables()), jnp.asarray(d_y_tables()),
        scratch=[pltpu.VMEM((ROWS, COLS), F32)],
        aliases={0: 0, 1: 1},
    )
    field = ((3, ROWS, COLS), F32)
    model, inside = call(
        halo_kernel,
        [half, half],
        1e9, 8,
        model, inside, before, after, left, right, jnp.asarray(d_halo_tables()),
        aliases={0: 0, 1: 1},
    )
    divergence, coefficient = call(
        scale_kernel,
        [field, ((lax.axis_size("gz"),), F32)],
        1e8, 8,
        model, inside, sums,
        out_specs=[VMEM, pl.BlockSpec(memory_space=pltpu.SMEM)],
    )
    return divergence[:, None], coefficient


def solution(mesh):
    return jax.shard_map(
        on_device,
        mesh=mesh,
        in_specs=(P(None, "gz", "gx", "gy"),),
        out_specs=(P(None, "gz", "gx", "gy"), P()),
        check_vma=False,
    )
```

```python
import functools

import jax
import jax.numpy as jnp
import ml_dtypes
import numpy as np
from jax import lax
from jax.experimental import pallas as pl
from jax.experimental.pallas import tpu as pltpu
from jax.sharding import PartitionSpec as P

ROWS = 512
COLS = 256
MARGIN = 32
HALO = 24
TILE = 128
WINDOW = TILE + 2 * MARGIN
INNER = ROWS - 2 * MARGIN
REACH = 64
POLE_F = -0.5
POLE_D = (np.sqrt(5.0) - 3.0) / 2.0
FIELDS = 11
OUTS = FIELDS + 3
NEAR = (3, 3, 3) + (2,) * 8
FAR = (2, 2, 2) + (1,) * 8
SLOTS = tuple(n + f for n, f in zip(NEAR, FAR))
START = tuple(int(s) for s in np.concatenate(([0], np.cumsum(SLOTS)[:-1])))
SENT = sum(SLOTS)
SENT_PAD = 40
DSENT = 2
BF = jnp.bfloat16
F32 = jnp.float32


def kernels(cells=2048):
    wave = 2.0 * np.pi * np.arange(cells // 2 + 1) / cells
    filt = (0.9375 + 0.89375 * np.cos(wave) - 0.0375 * np.cos(2 * wave) + 0.00625 * np.cos(3 * wave)) / (
        1.0 + 0.8 * np.cos(wave)
    )
    deri = 1j * (14.0 / 9.0 * np.sin(wave) + np.sin(2 * wave) / 18.0) / (1.0 + 2.0 / 3.0 * np.cos(wave))
    return tuple(np.fft.irfft(s, n=cells) for s in (filt, deri, deri * filt))


KF, KD, KG = kernels()


def split(table):
    high = np.asarray(table, np.float32).astype(ml_dtypes.bfloat16)
    low = (np.asarray(table, np.float64) - high.astype(np.float64)).astype(ml_dtypes.bfloat16)
    return high, low


def toeplitz(kernel, rows, cols, shift):
    offset = np.arange(rows)[:, None] + shift - np.arange(cols)[None, :]
    return kernel[offset % len(kernel)]


def left_operand(table):
    high, low = split(table)
    return np.concatenate([high, high, low], axis=1)


def right_operand(table):
    high, low = split(table)
    return np.concatenate([high, low], axis=0)


def thrice(table, cols=slice(None)):
    half = table.shape[0] // 2
    high, low = table[:half, cols], table[half:, cols]
    return jnp.concatenate([high, high, low], axis=0)


def far_fit(kernel, poles, near):
    k = np.arange(near + 1, near + 1 + len(poles))
    weight = np.linalg.solve(np.stack([np.power(p, k) for p in poles], axis=1), kernel[k])
    k = np.arange(1, near + 1)
    rest = kernel[k] - sum(w * np.power(p, k) for w, p in zip(weight, poles))
    return weight, rest


D_FAR, D_NEAR = [float(x[0]) for x in far_fit(KD, (POLE_D,), 1)]


def from_left(kernel, poles, near, slots_near, slots_far):
    weight, rest = far_fit(kernel, poles, near)
    table = np.zeros((slots_near + slots_far, COLS))
    for m in range(1, near + 1):
        for c in range(0, near - m + 1):
            table[m - 1, c] = rest[c + m - 1]
    for s, (w, p) in enumerate(zip(weight, poles)):
        table[slots_near + s] = w * np.power(p, np.arange(COLS, dtype=np.float64))
    return table


def send_table(near, far, poles):
    depth = 64
    table = np.zeros((depth, near + far))
    for m in range(near):
        table[m, m] = 1.0
    for s in range(far):
        table[:, near + s] = np.power(poles[s], np.arange(1, depth + 1, dtype=np.float64))
    return table


def edge_table(near, far, start, width=128, second=64):
    send = send_table(near, far, (POLE_F, POLE_D) if near > 1 else (POLE_D,))
    table = np.zeros((128, width))
    n = near + far
    table[64:, start : start + n] = send[::-1]
    table[:64, second + start : second + start + n] = send
    return table


def x_tables(tile):
    f = toeplitz(KF, tile, tile + 2 * MARGIN, MARGIN)
    g = toeplitz(KG, tile, tile + 2 * MARGIN, MARGIN)
    return left_operand(np.concatenate([f, g], axis=0))


def outer_tables():
    rows = []
    for kernel in (KG, KF):
        block = toeplitz(kernel, MARGIN, 3 * MARGIN, MARGIN)
        rows.append(split(np.kron(np.eye(2), block)))
    (g_high, g_low), (f_high, f_low) = rows
    return np.concatenate([g_high, f_high, f_low, g_low], axis=0)


def edge_tables():
    main, rest = [], []
    for i in range(0, FIELDS, 2):
        a, b = [edge_table(NEAR[k], FAR[k], START[k]) if k < FIELDS else np.zeros((128, 128)) for k in (i, i + 1)]
        high, low = split(np.concatenate([a[:32], b[96:], b[:32], a[96:]], axis=0))
        main.append(high)
        if i < 3:
            rest.append(low)
    return np.concatenate(main + rest, axis=0)


def edge_operand(edge, fields, low):
    block = [edge[pl.ds(i * 128, 128), :] for i in range(fields + low)]
    return jnp.concatenate([b for b in block[:fields] for _ in range(2)] + block[fields:], axis=0)


ORDER = np.concatenate([np.arange(64), np.arange(192, 256), np.arange(128, 192), np.arange(64, 128)])


def y_tables():
    f = toeplitz(KF, COLS, COLS, 0).T[:, ORDER]
    g = toeplitz(KG, COLS, COLS, 0).T[:, ORDER]
    return right_operand(np.concatenate([f, g], axis=1))


def halo_tables():
    table = np.zeros((2 * SENT, OUTS * 128))
    for out in range(OUTS):
        field = out if out < FIELDS else out - FIELDS
        if out < FIELDS:
            left = from_left(KF, (POLE_F,), 2, NEAR[field], FAR[field])
            if FAR[field] == 2:
                left[NEAR[field] + 1] = 0.0
            sign = 1.0
        else:
            left = from_left(KG, (POLE_F, POLE_D), 3, NEAR[field], FAR[field])
            sign = -1.0
        left = left[:, :REACH]
        start = START[field]
        table[start : start + SLOTS[field], out * 128 : out * 128 + REACH] = left
        table[SENT + start : SENT + start + SLOTS[field], out * 128 + REACH : (out + 1) * 128] = sign * left[:, ::-1]
    full = np.zeros((256, OUTS * 128), ml_dtypes.bfloat16)
    high, low = split(table)
    n = 2 * SENT
    full[:n], full[n : 2 * n], full[2 * n : 3 * n] = high, high, low
    return full


def d_edge_tables():
    main, rest = [], []
    for i in range(3):
        high, low = split(edge_table(1, 1, 2 * i, second=8))
        main.append(high)
        rest.append(low)
    return np.concatenate(main + rest, axis=0)


def d_halo_tables():
    table = np.zeros((16, 3 * 128))
    left = from_left(KD, (POLE_D,), 1, 1, 1)[:, :REACH]
    for out in range(3):
        table[2 * out : 2 * out + 2, out * 128 : out * 128 + REACH] = left
        table[8 + 2 * out : 8 + 2 * out + 2, out * 128 + REACH : (out + 1) * 128] = -left[:, ::-1]
    return right_operand(table)


def d_x_tables():
    return np.concatenate(split(toeplitz(KD, TILE, WINDOW, MARGIN)), axis=0)


def d_powers(length, sign=1.0):
    row = lax.broadcasted_iota(jnp.int32, (8, 1), 0)
    column = jnp.zeros((8, 1), F32)
    for s in range(8):
        power = POLE_D ** (s + 1) if sign > 0 else POLE_D ** (8 - s)
        column = jnp.where(row == s, float(power), column)
    blocks = range(length // 8) if sign > 0 else range(length // 8 - 1, -1, -1)
    return jnp.concatenate([column * float(POLE_D ** (8 * k)) for k in blocks], axis=0)


def d_y_tables():
    return right_operand(toeplitz(KD, COLS, COLS, 0).T[ORDER][:, ORDER])


def parts(value):
    high = value.astype(BF)
    return high, (value - high.astype(F32)).astype(BF)


def dot(a, b):
    return jnp.dot(a, b, preferred_element_type=F32)


def products_of(v):
    ww = v[2] * v[2]
    return [v[0] * v[0] - ww, v[1] * v[1] - ww, v[0] * v[1], v[0] * v[2], v[1] * v[2]]


def x_outer(table, high, low, both):
    tile = 2 * MARGIN
    if not both:
        a, b = dot(table[pl.ds(tile, 2 * tile), :], high), dot(table[pl.ds(tile, tile), :], low)
        return a[:tile] + (a[tile:] + b), None
    a, b = dot(table[...], high), dot(table[pl.ds(0, 2 * tile), :], low)
    return a[tile : 2 * tile] + (a[2 * tile : 3 * tile] + b[tile:]), a[:tile] + (a[3 * tile :] + b[:tile])


def x_inner(table, high, low, both):
    tile = table.shape[0] // 2
    stacked = jnp.concatenate([high, low, high], axis=0)
    if not both:
        return dot(table[pl.ds(0, tile), :], stacked), None
    done = dot(table[...], stacked)
    return done[:tile], done[tile:]


def x_tile(v, tile, apply, put, mixed, rows):
    data = v + products_of(v)
    done = [None] * FIELDS
    for i, value in enumerate(data):
        high, low = parts(value)
        f, g = apply(high, low, i < 3)
        if i < 3:
            done[i], done[3 + i] = f, g
        else:
            done[3 + i] = f
    lane = lax.broadcasted_iota(jnp.int32, (tile, 128), 1)
    edges = []
    for i, value in enumerate(done):
        put(i, *parts(value))
        edges.append(jnp.where(lane < 64, value[:, :128], value[:, 128:]))
    for i in range(0, FIELDS, 2):
        between = pltpu.roll(edges[i + 1], 64, 1) if i + 1 < FIELDS else 0.0
        both = jnp.where((lane < 32) | (lane >= 96), edges[i], between)
        high, low = parts(both)
        mixed[rows, pl.ds(128 * i, 128)] = high
        mixed[rows, pl.ds(128 * i + 128, 128)] = low
        if i < 3:
            mixed[rows, pl.ds(1536 + 64 * i, 128)] = high


def strip_kernel(first, last, first_out, last_out):
    first_out[...], last_out[...] = first[...], last[...]


WHOLE = INNER // 128 * 128


def middle_kernel(v, table, small, edge, out, sent, rest, mixed):
    at = 0
    while at < INNER:
        tile = min(TILE, INNER - at)
        rows = pl.ds(at, tile)

        def put(i, high, low):
            out[i, 0, rows, :] = high
            out[i, 1, rows, :] = low

        apply = functools.partial(x_inner, table if tile == TILE else small)
        x_tile([v[i, pl.ds(at, tile + 2 * MARGIN), :] for i in range(3)], tile, apply, put, mixed, rows)
        at += tile
    every = dot(mixed[...], edge_operand(edge, 6, 2))
    sent[...] = every[:WHOLE].T
    rest[...] = every[WHOLE:]


def outer_kernel(v, before, after, middle, rest, table, edge, out, to_right, to_left, mixed):
    none = jnp.zeros((MARGIN - HALO, COLS), F32)
    first, last = pl.ds(0, 2 * MARGIN), pl.ds(ROWS - 2 * MARGIN, 2 * MARGIN)
    values = [jnp.concatenate([none, before[i], v[i, first, :], v[i, last, :], after[i], none], axis=0) for i in range(3)]

    def put(i, high, low):
        out[i, 0] = high
        out[i, 1] = low

    x_tile(values, 2 * MARGIN, functools.partial(x_outer, table), put, mixed, pl.ds(0, 2 * MARGIN))
    sent = dot(mixed[...], edge_operand(edge, 6, 2))
    end = jnp.concatenate([rest[...], sent], axis=0).T
    for target, start in ((to_right, 0), (to_left, 64)):
        target[:, pl.ds(0, WHOLE)] = middle[pl.ds(start, SENT_PAD), :]
        target[:, pl.ds(WHOLE, ROWS - WHOLE)] = end[start : start + SENT_PAD]


CHUNK = 16


def stress(f, pair_sums):
    smooth, gx, products, gy = f[0:3], f[3:6], f[6:11], f[11:14]
    sxx, syy = gx[0], gy[1]
    szz = -(sxx + syy)
    sxy = 0.5 * (gy[0] + gx[1])
    sxz = 0.5 * gx[2]
    syz = 0.5 * gy[2]
    inner = sxx * sxx + syy * syy + szz * szz + 2.0 * (sxy * sxy + sxz * sxz + syz * syz)
    magnitude = jnp.sqrt(2.0 * inner)
    strain = (sxx, sxy, sxz, syy, syz)
    leonard = [product - own for product, own in zip(products, products_of(smooth))]
    single = leonard[0] * sxx + leonard[1] * syy
    double = leonard[2] * sxy + leonard[3] * sxz + leonard[4] * syz
    pair_sums[0] += (single + 2.0 * double) * magnitude
    pair_sums[1] += 2.0 * inner * inner
    return [magnitude * strain[i] for i in range(5)]


def y_kernel(middle, outer, table, out, model, pair_sums, held):
    for i in range(FIELDS):
        high, low = [
            jnp.concatenate(
                [outer[i, k, pl.ds(0, MARGIN), :], middle[i, k], outer[i, k, pl.ds(MARGIN, MARGIN), :]], axis=0
            )
            for k in range(2)
        ]
        data = jnp.concatenate([high, low, high], axis=1)
        done = dot(data, thrice(table) if i < 3 else thrice(table, slice(0, COLS)))
        out[i], held[i] = done[:, :128], done[:, 128:COLS]
        if i < 3:
            out[FIELDS + i], held[FIELDS + i] = done[:, COLS : COLS + 128], done[:, COLS + 128 :]
    pair_sums[...] = jnp.zeros_like(pair_sums)

    def chunk(step, carry):
        rows = pl.ds(pl.multiple_of(step * CHUNK, CHUNK), CHUNK)
        for i, value in enumerate(stress([held[k, rows, :] for k in range(OUTS)], pair_sums)):
            model[i, rows, :] = value
        return carry

    lax.fori_loop(0, ROWS // CHUNK, chunk, 0, unroll=4)


def model_kernel(
    local, inside_sums, left, right, table, model, sums, halo, added, total
):
    high, low = parts(left[...])
    high2, low2 = parts(right[...])
    n = SENT
    halo[pl.ds(6 * SENT, 256 - 6 * SENT), :] = jnp.zeros((256 - 6 * SENT, ROWS), F32)
    for k, (a, b) in enumerate(((high, high2), (low, low2), (high, high2))):
        halo[pl.ds(2 * n * k, n), :] = a.astype(F32)[:n]
        halo[pl.ds(2 * n * k + n, n), :] = b.astype(F32)[:n]
    total[...] = inside_sums[...]
    done = dot(halo[...].T.astype(BF), table[...])
    added[pl.ds(MARGIN, INNER), :] = done[:INNER]
    added[pl.ds(0, MARGIN), :] = done[INNER : INNER + MARGIN]
    added[pl.ds(MARGIN + INNER, MARGIN), :] = done[INNER + MARGIN :]

    def chunk(step, carry):
        rows = pl.ds(pl.multiple_of(step * CHUNK, CHUNK), CHUNK)
        f = [local[i, rows, :] + added[rows, pl.ds(i * 128, 128)] for i in range(OUTS)]
        for i, value in enumerate(stress(f, total)):
            model[i, rows, :] = value
        return carry

    lax.fori_loop(0, ROWS // CHUNK, chunk, 0, unroll=4)
    cross, square = jnp.sum(total[0]), jnp.sum(total[1])
    lane = lax.broadcasted_iota(jnp.int32, sums.shape, 1)
    sums[...] = jnp.where(lane < 64, cross, square)


def send_kernel(model, inside, edge, first, last, to_right, to_left):
    main, rest = [], []
    for i in (1, 3, 4):
        high, low = parts(model[i])
        main += [high, low]
        rest.append(high)
    sent = dot(jnp.concatenate(main + rest, axis=1), edge_operand(edge, 3, 3)).T
    to_right[...] = sent[:8]
    to_left[...] = sent[8:16]
    near_first, near_last = d_powers(MARGIN), d_powers(MARGIN, -1.0)
    first[...] = jnp.zeros_like(first)
    last[...] = jnp.zeros_like(last)
    for k, source in enumerate((model, inside)):
        lanes = pl.ds(128 * k, 128)
        for i in range(3):
            low, high = source[i, pl.ds(0, MARGIN), :], source[i, pl.ds(ROWS - MARGIN, MARGIN), :]
            first[i : i + 1, lanes] = low[:1]
            last[i : i + 1, lanes] = high[MARGIN - 1 :]
            first[i + 3 : i + 4, lanes] = jnp.sum(near_first * low, axis=0, keepdims=True)
            last[i + 3 : i + 4, lanes] = jnp.sum(near_last * high, axis=0, keepdims=True)


def local_kernel(edge, inside, xt, yt, edge_out, inside_out, held):
    none = jnp.zeros((MARGIN, COLS), F32)

    def model(i, start, length):
        rows = pl.ds(start, length)
        return jnp.concatenate([edge[i, rows, :], inside[i, rows, :]], axis=1)

    for c, (i, j) in enumerate(((0, 1), (1, 3), (2, 4))):
        high, low = parts(model(j, 0, ROWS))
        along_y = dot(jnp.concatenate([high, low, high], axis=1), thrice(yt))
        for start in range(0, ROWS, TILE):
            tile = min(TILE, ROWS - start)
            rows = pl.ds(start, tile)
            begin, end = max(start - MARGIN, 0), min(start + TILE + MARGIN, ROWS)
            window = model(i, begin, end - begin)
            if begin == 0:
                window = jnp.concatenate([none, window], axis=0)
            if window.shape[0] < WINDOW:
                window = jnp.concatenate([window, jnp.zeros((WINDOW - window.shape[0], COLS), F32)], axis=0)
            high, low = parts(window)
            a, b = dot(xt[...], high), dot(xt[pl.ds(0, TILE), :], low)
            both = (a[:tile] + (a[TILE : TILE + tile] + b[:tile])) + along_y[start : start + tile]
            if c == 0:
                held[rows, :] = both
            else:
                edge_out[j, rows, :], inside_out[j, rows, :] = both[:, :128], both[:, 128:]
    edge_out[0], inside_out[0] = held[:, pl.ds(0, 128)], held[:, pl.ds(128, 128)]


def halo_kernel(edge, inside, before, after, left, right, ht, edge_out, inside_out):
    halo = jnp.concatenate([left[...], right[...], jnp.zeros((112, ROWS), F32)], axis=0)
    high, low = parts(halo.T)
    high, low = high[:, :16], low[:, :16]
    added = dot(jnp.concatenate([high, low, high], axis=1), thrice(ht))
    row = lax.broadcasted_iota(jnp.int32, (MARGIN, 1), 0)
    for c, i in enumerate((0, 3, 4)):
        edge_out[i] = edge[i] + added[:, c * 128 : (c + 1) * 128]
        inside_out[i] = inside[i]
        for strip, sign, start in ((before, 1.0, 0), (after, -1.0, ROWS - MARGIN)):
            decay = d_powers(MARGIN, sign) * float(sign * D_FAR / POLE_D)
            near = jnp.where(row == (0 if start == 0 else MARGIN - 1), sign * D_NEAR * strip[c : c + 1], 0.0)
            part = decay * strip[c + 3 : c + 4] + near
            rows = pl.ds(start, MARGIN)
            edge_out[i, rows, :] += part[:, :128]
            inside_out[i, rows, :] += part[:, 128:]


def scale_kernel(edge, inside, sums, out, coefficient):
    groups = coefficient.shape[0]
    part = sums[...]
    plane = lax.broadcasted_iota(jnp.int32, part.shape, 0) % groups
    at = lax.axis_index("gz")
    scale = jnp.zeros((1, 1), F32)
    ratios = []
    for g in range(groups):
        mean = jnp.sum(jnp.where(plane == g, part, 0.0), axis=0, keepdims=True) * (
            groups / (part.shape[0] * ROWS * COLS)
        )
        ratios.append(mean[:, 0:1] / (mean[:, 64:65] + 1e-06))
        scale = jnp.where(at == g, ratios[g], scale)
    outer = lax.broadcasted_iota(jnp.int32, (ROWS, 128), 1) < 64
    for c, i in enumerate((0, 3, 4)):
        e, m = scale * edge[i], scale * inside[i]
        out[c, :, pl.ds(0, 128)] = jnp.where(outer, e, m)
        out[c, :, pl.ds(128, 128)] = jnp.where(outer, m, e)
    for g in range(groups):
        coefficient[g] = ratios[g][0, 0]


VMEM = pl.BlockSpec(memory_space=pltpu.VMEM)


def call(kernel, outs, flops, limit, *args, scratch=(), out_specs=None, aliases=None):
    return pl.pallas_call(
        kernel,
        out_shape=[jax.ShapeDtypeStruct(s, d) for s, d in outs],
        in_specs=[VMEM] * len(args),
        out_specs=out_specs or [VMEM] * len(outs),
        scratch_shapes=list(scratch),
        input_output_aliases=aliases or {},
        cost_estimate=pl.CostEstimate(flops=int(flops), bytes_accessed=6 << 20, transcendentals=0),
        compiler_params=pltpu.CompilerParams(vmem_limit_bytes=limit << 20),
    )(*args)


def exchange(to_next, to_previous, axis):
    n = lax.axis_size(axis)
    up = [(i, (i + 1) % n) for i in range(n)]
    down = [(j, i) for i, j in up]
    return lax.ppermute(to_next, axis, up), lax.ppermute(to_previous, axis, down)


def on_device(velocity):
    v = velocity[:, 0]
    edge = jnp.asarray(edge_tables())
    strip = ((3, HALO, COLS), F32)
    first, last = call(strip_kernel, [strip, strip], 2e11, 2, v[:, :HALO], v[:, ROWS - HALO :])
    before, after = exchange(last, first, "gx")
    middle, sent, rest = call(
        middle_kernel,
        [((FIELDS, 2, INNER, COLS), BF), ((128, WHOLE), F32), ((INNER - WHOLE, 128), F32)],
        4e9, 10,
        v, jnp.asarray(x_tables(TILE)), jnp.asarray(x_tables(INNER % TILE)), edge,
        scratch=[pltpu.VMEM((INNER, 1792), BF)],
    )
    outer, to_right, to_left = call(
        outer_kernel,
        [((FIELDS, 2, 2 * MARGIN, COLS), BF), ((SENT_PAD, ROWS), F32), ((SENT_PAD, ROWS), F32)],
        1e9, 8,
        v, before, after, sent, rest, jnp.asarray(outer_tables()), edge,
        scratch=[pltpu.VMEM((2 * MARGIN, 1792), BF)],
    )
    left, right = exchange(to_right, to_left, "gy")
    half = ((5, ROWS, 128), F32)
    local, inside, inside_sums = call(
        y_kernel,
        [((OUTS, ROWS, 128), F32), half, ((2, CHUNK, 128), F32)],
        4e9, 12,
        middle, outer, jnp.asarray(y_tables()),
        scratch=[pltpu.VMEM((OUTS, ROWS, 128), F32)],
    )
    devices = lax.axis_size("gx") * lax.axis_size("gy") * lax.axis_size("gz")
    model, sums = call(
        model_kernel,
        [half, ((devices, 128), F32)],
        4e9, 12,
        local, inside_sums, left, right, jnp.asarray(halo_tables()),
        scratch=[
            pltpu.VMEM((256, ROWS), F32),
            pltpu.VMEM((ROWS, OUTS * 128), F32),
            pltpu.VMEM((2, CHUNK, 128), F32),
        ],
    )
    sums = lax.all_to_all(sums, ("gx", "gy", "gz"), 0, 0, tiled=True)
    first, last, to_right, to_left = call(
        send_kernel,
        [((8, COLS), F32), ((8, COLS), F32), ((8, ROWS), F32), ((8, ROWS), F32)],
        1e8, 4,
        model, inside, jnp.asarray(d_edge_tables()),
    )
    before, after = exchange(last, first, "gx")
    left, right = exchange(to_right, to_left, "gy")
    model, inside = call(
        local_kernel,
        [half, half],
        4e9, 8,
        model, inside, jnp.asarray(d_x_tables()), jnp.asarray(d_y_tables()),
        scratch=[pltpu.VMEM((ROWS, COLS), F32)],
        aliases={0: 0, 1: 1},
    )
    field = ((3, ROWS, COLS), F32)
    model, inside = call(
        halo_kernel,
        [half, half],
        1e9, 8,
        model, inside, before, after, left, right, jnp.asarray(d_halo_tables()),
        aliases={0: 0, 1: 1},
    )
    divergence, coefficient = call(
        scale_kernel,
        [field, ((lax.axis_size("gz"),), F32)],
        1e8, 8,
        model, inside, sums,
        out_specs=[VMEM, pl.BlockSpec(memory_space=pltpu.SMEM)],
    )
    return divergence[:, None], coefficient


def solution(mesh):
    return jax.shard_map(
        on_device,
        mesh=mesh,
        in_specs=(P(None, "gz", "gx", "gy"),),
        out_specs=(P(None, "gz", "gx", "gy"), P()),
        check_vma=False,
    )
```

```python
import functools

import jax
import jax.numpy as jnp
import ml_dtypes
import numpy as np
from jax import lax
from jax.experimental import pallas as pl
from jax.experimental.pallas import tpu as pltpu
from jax.sharding import PartitionSpec as P

ROWS = 512
COLS = 256
MARGIN = 32
HALO = 24
TILE = 128
WINDOW = TILE + 2 * MARGIN
INNER = ROWS - 2 * MARGIN
REACH = 64
POLE_F = -0.5
POLE_D = (np.sqrt(5.0) - 3.0) / 2.0
FIELDS = 11
OUTS = FIELDS + 3
NEAR = (3, 3, 3) + (2,) * 8
FAR = (2, 2, 2) + (1,) * 8
SLOTS = tuple(n + f for n, f in zip(NEAR, FAR))
START = tuple(int(s) for s in np.concatenate(([0], np.cumsum(SLOTS)[:-1])))
SENT = sum(SLOTS)
SENT_PAD = 40
DSENT = 2
BF = jnp.bfloat16
F32 = jnp.float32


def kernels(cells=2048):
    wave = 2.0 * np.pi * np.arange(cells // 2 + 1) / cells
    filt = (0.9375 + 0.89375 * np.cos(wave) - 0.0375 * np.cos(2 * wave) + 0.00625 * np.cos(3 * wave)) / (
        1.0 + 0.8 * np.cos(wave)
    )
    deri = 1j * (14.0 / 9.0 * np.sin(wave) + np.sin(2 * wave) / 18.0) / (1.0 + 2.0 / 3.0 * np.cos(wave))
    return tuple(np.fft.irfft(s, n=cells) for s in (filt, deri, deri * filt))


KF, KD, KG = kernels()


def split(table):
    high = np.asarray(table, np.float32).astype(ml_dtypes.bfloat16)
    low = (np.asarray(table, np.float64) - high.astype(np.float64)).astype(ml_dtypes.bfloat16)
    return high, low


def toeplitz(kernel, rows, cols, shift):
    offset = np.arange(rows)[:, None] + shift - np.arange(cols)[None, :]
    return kernel[offset % len(kernel)]


def left_operand(table):
    high, low = split(table)
    return np.concatenate([high, high, low], axis=1)


def right_operand(table):
    high, low = split(table)
    return np.concatenate([high, low], axis=0)


def thrice(table, cols=slice(None)):
    half = table.shape[0] // 2
    high, low = table[:half, cols], table[half:, cols]
    return jnp.concatenate([high, high, low], axis=0)


def far_fit(kernel, poles, near):
    k = np.arange(near + 1, near + 1 + len(poles))
    weight = np.linalg.solve(np.stack([np.power(p, k) for p in poles], axis=1), kernel[k])
    k = np.arange(1, near + 1)
    rest = kernel[k] - sum(w * np.power(p, k) for w, p in zip(weight, poles))
    return weight, rest


D_FAR, D_NEAR = [float(x[0]) for x in far_fit(KD, (POLE_D,), 1)]


def from_left(kernel, poles, near, slots_near, slots_far):
    weight, rest = far_fit(kernel, poles, near)
    table = np.zeros((slots_near + slots_far, COLS))
    for m in range(1, near + 1):
        for c in range(0, near - m + 1):
            table[m - 1, c] = rest[c + m - 1]
    for s, (w, p) in enumerate(zip(weight, poles)):
        table[slots_near + s] = w * np.power(p, np.arange(COLS, dtype=np.float64))
    return table


def send_table(near, far, poles):
    depth = 64
    table = np.zeros((depth, near + far))
    for m in range(near):
        table[m, m] = 1.0
    for s in range(far):
        table[:, near + s] = np.power(poles[s], np.arange(1, depth + 1, dtype=np.float64))
    return table


def edge_table(near, far, start, width=128, second=64):
    send = send_table(near, far, (POLE_F, POLE_D) if near > 1 else (POLE_D,))
    table = np.zeros((128, width))
    n = near + far
    table[64:, start : start + n] = send[::-1]
    table[:64, second + start : second + start + n] = send
    return table


def x_tables(tile):
    f = toeplitz(KF, tile, tile + 2 * MARGIN, MARGIN)
    g = toeplitz(KG, tile, tile + 2 * MARGIN, MARGIN)
    return left_operand(np.concatenate([f, g], axis=0))


def outer_tables():
    rows = []
    for kernel in (KG, KF):
        block = toeplitz(kernel, MARGIN, 3 * MARGIN, MARGIN)
        rows.append(split(np.kron(np.eye(2), block)))
    (g_high, g_low), (f_high, f_low) = rows
    return np.concatenate([g_high, f_high, f_low, g_low], axis=0)


def edge_tables():
    main, rest = [], []
    for i in range(0, FIELDS, 2):
        a, b = [edge_table(NEAR[k], FAR[k], START[k]) if k < FIELDS else np.zeros((128, 128)) for k in (i, i + 1)]
        high, low = split(np.concatenate([a[:32], b[96:], b[:32], a[96:]], axis=0))
        main.append(high)
        if i < 3:
            rest.append(low)
    return np.concatenate(main + rest, axis=0)


def edge_operand(edge, fields, low):
    block = [edge[pl.ds(i * 128, 128), :] for i in range(fields + low)]
    return jnp.concatenate([b for b in block[:fields] for _ in range(2)] + block[fields:], axis=0)


ORDER = np.concatenate([np.arange(64), np.arange(192, 256), np.arange(128, 192), np.arange(64, 128)])


def y_tables():
    f = toeplitz(KF, COLS, COLS, 0).T[:, ORDER]
    g = toeplitz(KG, COLS, COLS, 0).T[:, ORDER]
    return right_operand(np.concatenate([f, g], axis=1))


def halo_tables():
    table = np.zeros((2 * SENT, OUTS * 128))
    for out in range(OUTS):
        field = out if out < FIELDS else out - FIELDS
        if out < FIELDS:
            left = from_left(KF, (POLE_F,), 2, NEAR[field], FAR[field])
            if FAR[field] == 2:
                left[NEAR[field] + 1] = 0.0
            sign = 1.0
        else:
            left = from_left(KG, (POLE_F, POLE_D), 3, NEAR[field], FAR[field])
            sign = -1.0
        left = left[:, :REACH]
        start = START[field]
        table[start : start + SLOTS[field], out * 128 : out * 128 + REACH] = left
        table[SENT + start : SENT + start + SLOTS[field], out * 128 + REACH : (out + 1) * 128] = sign * left[:, ::-1]
    full = np.zeros((256, OUTS * 128), ml_dtypes.bfloat16)
    high, low = split(table)
    n = 2 * SENT
    full[:n], full[n : 2 * n], full[2 * n : 3 * n] = high, high, low
    return full


def d_edge_tables():
    main, rest = [], []
    for i in range(3):
        high, low = split(edge_table(1, 1, 2 * i, second=8))
        main.append(high)
        rest.append(low)
    return np.concatenate(main + rest, axis=0)


def d_halo_tables():
    table = np.zeros((16, 3 * 128))
    left = from_left(KD, (POLE_D,), 1, 1, 1)[:, :REACH]
    for out in range(3):
        table[2 * out : 2 * out + 2, out * 128 : out * 128 + REACH] = left
        table[8 + 2 * out : 8 + 2 * out + 2, out * 128 + REACH : (out + 1) * 128] = -left[:, ::-1]
    return right_operand(table)


def d_x_tables():
    return np.concatenate(split(toeplitz(KD, TILE, WINDOW, MARGIN)), axis=0)


def d_powers(length, sign=1.0):
    row = lax.broadcasted_iota(jnp.int32, (8, 1), 0)
    column = jnp.zeros((8, 1), F32)
    for s in range(8):
        power = POLE_D ** (s + 1) if sign > 0 else POLE_D ** (8 - s)
        column = jnp.where(row == s, float(power), column)
    blocks = range(length // 8) if sign > 0 else range(length // 8 - 1, -1, -1)
    return jnp.concatenate([column * float(POLE_D ** (8 * k)) for k in blocks], axis=0)


def d_y_tables():
    return right_operand(toeplitz(KD, COLS, COLS, 0).T[ORDER][:, ORDER])


def parts(value):
    high = value.astype(BF)
    return high, (value - high.astype(F32)).astype(BF)


def dot(a, b):
    return jnp.dot(a, b, preferred_element_type=F32)


def products_of(v):
    ww = v[2] * v[2]
    return [v[0] * v[0] - ww, v[1] * v[1] - ww, v[0] * v[1], v[0] * v[2], v[1] * v[2]]


def x_outer(table, high, low, both):
    tile = 2 * MARGIN
    if not both:
        a, b = dot(table[pl.ds(tile, 2 * tile), :], high), dot(table[pl.ds(tile, tile), :], low)
        return a[:tile] + (a[tile:] + b), None
    a, b = dot(table[...], high), dot(table[pl.ds(0, 2 * tile), :], low)
    return a[tile : 2 * tile] + (a[2 * tile : 3 * tile] + b[tile:]), a[:tile] + (a[3 * tile :] + b[:tile])


def x_inner(table, high, low, both):
    tile = table.shape[0] // 2
    stacked = jnp.concatenate([high, low, high], axis=0)
    if not both:
        return dot(table[pl.ds(0, tile), :], stacked), None
    done = dot(table[...], stacked)
    return done[:tile], done[tile:]


def x_tile(v, tile, apply, put, mixed, rows):
    data = v + products_of(v)
    done = [None] * FIELDS
    for i, value in enumerate(data):
        high, low = parts(value)
        f, g = apply(high, low, i < 3)
        if i < 3:
            done[i], done[3 + i] = f, g
        else:
            done[3 + i] = f
    lane = lax.broadcasted_iota(jnp.int32, (tile, 128), 1)
    edges = []
    for i, value in enumerate(done):
        put(i, *parts(value))
        edges.append(jnp.where(lane < 64, value[:, :128], value[:, 128:]))
    for i in range(0, FIELDS, 2):
        between = pltpu.roll(edges[i + 1], 64, 1) if i + 1 < FIELDS else 0.0
        both = jnp.where((lane < 32) | (lane >= 96), edges[i], between)
        high, low = parts(both)
        mixed[rows, pl.ds(128 * i, 128)] = high
        mixed[rows, pl.ds(128 * i + 128, 128)] = low
        if i < 3:
            mixed[rows, pl.ds(1536 + 64 * i, 128)] = high


def strip_kernel(first, last, first_out, last_out):
    first_out[...], last_out[...] = first[...], last[...]


WHOLE = INNER // 128 * 128


def middle_kernel(v, table, small, edge, out, sent, rest, mixed):
    at = 0
    while at < INNER:
        tile = min(TILE, INNER - at)
        rows = pl.ds(at, tile)

        def put(i, high, low):
            out[i, 0, rows, :] = high
            out[i, 1, rows, :] = low

        apply = functools.partial(x_inner, table if tile == TILE else small)
        x_tile([v[i, pl.ds(at, tile + 2 * MARGIN), :] for i in range(3)], tile, apply, put, mixed, rows)
        at += tile
    every = dot(mixed[...], edge_operand(edge, 6, 2))
    sent[...] = every[:WHOLE].T
    rest[...] = every[WHOLE:]


def outer_kernel(v, before, after, middle, rest, table, edge, out, to_right, to_left, mixed):
    none = jnp.zeros((MARGIN - HALO, COLS), F32)
    first, last = pl.ds(0, 2 * MARGIN), pl.ds(ROWS - 2 * MARGIN, 2 * MARGIN)
    values = [jnp.concatenate([none, before[i], v[i, first, :], v[i, last, :], after[i], none], axis=0) for i in range(3)]

    def put(i, high, low):
        out[i, 0] = high
        out[i, 1] = low

    x_tile(values, 2 * MARGIN, functools.partial(x_outer, table), put, mixed, pl.ds(0, 2 * MARGIN))
    sent = dot(mixed[...], edge_operand(edge, 6, 2))
    end = jnp.concatenate([rest[...], sent], axis=0).T
    for target, start in ((to_right, 0), (to_left, 64)):
        target[:, pl.ds(0, WHOLE)] = middle[pl.ds(start, SENT_PAD), :]
        target[:, pl.ds(WHOLE, ROWS - WHOLE)] = end[start : start + SENT_PAD]


CHUNK = 16


def stress(f, pair_sums):
    smooth, gx, products, gy = f[0:3], f[3:6], f[6:11], f[11:14]
    sxx, syy = gx[0], gy[1]
    szz = -(sxx + syy)
    sxy = 0.5 * (gy[0] + gx[1])
    sxz = 0.5 * gx[2]
    syz = 0.5 * gy[2]
    inner = sxx * sxx + syy * syy + szz * szz + 2.0 * (sxy * sxy + sxz * sxz + syz * syz)
    magnitude = jnp.sqrt(2.0 * inner)
    strain = (sxx, sxy, sxz, syy, syz)
    leonard = [product - own for product, own in zip(products, products_of(smooth))]
    single = leonard[0] * sxx + leonard[1] * syy
    double = leonard[2] * sxy + leonard[3] * sxz + leonard[4] * syz
    pair_sums[0] += (single + 2.0 * double) * magnitude
    pair_sums[1] += 2.0 * inner * inner
    return [magnitude * strain[i] for i in range(5)]


def y_kernel(middle, outer, table, out, model, pair_sums, held):
    for i in range(FIELDS):
        high, low = [
            jnp.concatenate(
                [outer[i, k, pl.ds(0, MARGIN), :], middle[i, k], outer[i, k, pl.ds(MARGIN, MARGIN), :]], axis=0
            )
            for k in range(2)
        ]
        data = jnp.concatenate([high, low, high], axis=1)
        done = dot(data, thrice(table) if i < 3 else thrice(table, slice(0, COLS)))
        out[i], held[i] = done[:, :128], done[:, 128:COLS]
        if i < 3:
            out[FIELDS + i], held[FIELDS + i] = done[:, COLS : COLS + 128], done[:, COLS + 128 :]
    pair_sums[...] = jnp.zeros_like(pair_sums)

    def chunk(step, carry):
        rows = pl.ds(pl.multiple_of(step * CHUNK, CHUNK), CHUNK)
        for i, value in enumerate(stress([held[k, rows, :] for k in range(OUTS)], pair_sums)):
            model[i, rows, :] = value
        return carry

    lax.fori_loop(0, ROWS // CHUNK, chunk, 0, unroll=4)


def model_kernel(
    local, inside_sums, left, right, table, model, sums, halo, added, total
):
    high, low = parts(left[...])
    high2, low2 = parts(right[...])
    n = SENT
    halo[pl.ds(6 * SENT, 256 - 6 * SENT), :] = jnp.zeros((256 - 6 * SENT, ROWS), F32)
    for k, (a, b) in enumerate(((high, high2), (low, low2), (high, high2))):
        halo[pl.ds(2 * n * k, n), :] = a.astype(F32)[:n]
        halo[pl.ds(2 * n * k + n, n), :] = b.astype(F32)[:n]
    total[...] = inside_sums[...]
    done = dot(halo[...].T.astype(BF), table[...])
    added[pl.ds(MARGIN, INNER), :] = done[:INNER]
    added[pl.ds(0, MARGIN), :] = done[INNER : INNER + MARGIN]
    added[pl.ds(MARGIN + INNER, MARGIN), :] = done[INNER + MARGIN :]

    def chunk(step, carry):
        rows = pl.ds(pl.multiple_of(step * CHUNK, CHUNK), CHUNK)
        f = [local[i, rows, :] + added[rows, pl.ds(i * 128, 128)] for i in range(OUTS)]
        for i, value in enumerate(stress(f, total)):
            model[i, rows, :] = value
        return carry

    lax.fori_loop(0, ROWS // CHUNK, chunk, 0, unroll=4)
    cross, square = jnp.sum(total[0]), jnp.sum(total[1])
    lane = lax.broadcasted_iota(jnp.int32, sums.shape, 1)
    sums[...] = jnp.where(lane < 64, cross, square)


def send_kernel(model, inside, edge, first, last, to_right, to_left):
    main, rest = [], []
    for i in (1, 3, 4):
        high, low = parts(model[i])
        main += [high, low]
        rest.append(high)
    sent = dot(jnp.concatenate(main + rest, axis=1), edge_operand(edge, 3, 3)).T
    to_right[...] = sent[:8]
    to_left[...] = sent[8:16]
    near_first, near_last = d_powers(MARGIN), d_powers(MARGIN, -1.0)
    first[...] = jnp.zeros_like(first)
    last[...] = jnp.zeros_like(last)
    for k, source in enumerate((model, inside)):
        lanes = pl.ds(128 * k, 128)
        for i in range(3):
            low, high = source[i, pl.ds(0, MARGIN), :], source[i, pl.ds(ROWS - MARGIN, MARGIN), :]
            first[i : i + 1, lanes] = low[:1]
            last[i : i + 1, lanes] = high[MARGIN - 1 :]
            first[i + 3 : i + 4, lanes] = jnp.sum(near_first * low, axis=0, keepdims=True)
            last[i + 3 : i + 4, lanes] = jnp.sum(near_last * high, axis=0, keepdims=True)


def local_kernel(edge, inside, xt, yt, edge_out, inside_out, held):
    none = jnp.zeros((MARGIN, COLS), F32)

    def model(i, start, length):
        rows = pl.ds(start, length)
        return jnp.concatenate([edge[i, rows, :], inside[i, rows, :]], axis=1)

    for c, (i, j) in enumerate(((0, 1), (1, 3), (2, 4))):
        high, low = parts(model(j, 0, ROWS))
        along_y = dot(jnp.concatenate([high, low, high], axis=1), thrice(yt))
        for start in range(0, ROWS, TILE):
            tile = min(TILE, ROWS - start)
            rows = pl.ds(start, tile)
            begin, end = max(start - MARGIN, 0), min(start + TILE + MARGIN, ROWS)
            window = model(i, begin, end - begin)
            if begin == 0:
                window = jnp.concatenate([none, window], axis=0)
            if window.shape[0] < WINDOW:
                window = jnp.concatenate([window, jnp.zeros((WINDOW - window.shape[0], COLS), F32)], axis=0)
            high, low = parts(window)
            a, b = dot(xt[...], high), dot(xt[pl.ds(0, TILE), :], low)
            both = (a[:tile] + (a[TILE : TILE + tile] + b[:tile])) + along_y[start : start + tile]
            if c == 0:
                held[rows, :] = both
            else:
                edge_out[j, rows, :], inside_out[j, rows, :] = both[:, :128], both[:, 128:]
    edge_out[0], inside_out[0] = held[:, pl.ds(0, 128)], held[:, pl.ds(128, 128)]


def halo_kernel(edge, inside, before, after, left, right, ht, edge_out, inside_out):
    halo = jnp.concatenate([left[...], right[...], jnp.zeros((112, ROWS), F32)], axis=0)
    high, low = parts(halo.T)
    high, low = high[:, :16], low[:, :16]
    added = dot(jnp.concatenate([high, low, high], axis=1), thrice(ht))
    row = lax.broadcasted_iota(jnp.int32, (MARGIN, 1), 0)
    for c, i in enumerate((0, 3, 4)):
        edge_out[i] = edge[i] + added[:, c * 128 : (c + 1) * 128]
        inside_out[i] = inside[i]
        for strip, sign, start in ((before, 1.0, 0), (after, -1.0, ROWS - MARGIN)):
            decay = d_powers(MARGIN, sign) * float(sign * D_FAR / POLE_D)
            near = jnp.where(row == (0 if start == 0 else MARGIN - 1), sign * D_NEAR * strip[c : c + 1], 0.0)
            part = decay * strip[c + 3 : c + 4] + near
            rows = pl.ds(start, MARGIN)
            edge_out[i, rows, :] += part[:, :128]
            inside_out[i, rows, :] += part[:, 128:]


def scale_kernel(edge, inside, sums, out, coefficient):
    groups = coefficient.shape[0]
    part = sums[...]
    plane = lax.broadcasted_iota(jnp.int32, part.shape, 0) % groups
    at = lax.axis_index("gz")
    scale = jnp.zeros((1, 1), F32)
    ratios = []
    for g in range(groups):
        mean = jnp.sum(jnp.where(plane == g, part, 0.0), axis=0, keepdims=True) * (
            groups / (part.shape[0] * ROWS * COLS)
        )
        ratios.append(mean[:, 0:1] / (mean[:, 64:65] + 1e-06))
        scale = jnp.where(at == g, ratios[g], scale)
    outer = lax.broadcasted_iota(jnp.int32, (ROWS, 128), 1) < 64
    for c, i in enumerate((0, 3, 4)):
        e, m = scale * edge[i], scale * inside[i]
        out[c, :, pl.ds(0, 128)] = jnp.where(outer, e, m)
        out[c, :, pl.ds(128, 128)] = jnp.where(outer, m, e)
    for g in range(groups):
        coefficient[g] = ratios[g][0, 0]


VMEM = pl.BlockSpec(memory_space=pltpu.VMEM)


def call(kernel, outs, flops, limit, *args, scratch=(), out_specs=None, aliases=None):
    return pl.pallas_call(
        kernel,
        out_shape=[jax.ShapeDtypeStruct(s, d) for s, d in outs],
        in_specs=[VMEM] * len(args),
        out_specs=out_specs or [VMEM] * len(outs),
        scratch_shapes=list(scratch),
        input_output_aliases=aliases or {},
        cost_estimate=pl.CostEstimate(flops=int(flops), bytes_accessed=6 << 20, transcendentals=0),
        compiler_params=pltpu.CompilerParams(vmem_limit_bytes=limit << 20),
    )(*args)


def exchange(to_next, to_previous, axis):
    n = lax.axis_size(axis)
    up = [(i, (i + 1) % n) for i in range(n)]
    down = [(j, i) for i, j in up]
    return lax.ppermute(to_next, axis, up), lax.ppermute(to_previous, axis, down)


def on_device(velocity):
    v = velocity[:, 0]
    edge = jnp.asarray(edge_tables())
    strip = ((3, HALO, COLS), F32)
    first, last = call(strip_kernel, [strip, strip], 2e11, 2, v[:, :HALO], v[:, ROWS - HALO :])
    before, after = exchange(last, first, "gx")
    middle, sent, rest = call(
        middle_kernel,
        [((FIELDS, 2, INNER, COLS), BF), ((128, WHOLE), F32), ((INNER - WHOLE, 128), F32)],
        4e9, 10,
        v, jnp.asarray(x_tables(TILE)), jnp.asarray(x_tables(INNER % TILE)), edge,
        scratch=[pltpu.VMEM((INNER, 1792), BF)],
    )
    outer, to_right, to_left = call(
        outer_kernel,
        [((FIELDS, 2, 2 * MARGIN, COLS), BF), ((SENT_PAD, ROWS), F32), ((SENT_PAD, ROWS), F32)],
        1e9, 8,
        v, before, after, sent, rest, jnp.asarray(outer_tables()), edge,
        scratch=[pltpu.VMEM((2 * MARGIN, 1792), BF)],
    )
    left, right = exchange(to_right, to_left, "gy")
    half = ((5, ROWS, 128), F32)
    local, inside, inside_sums = call(
        y_kernel,
        [((OUTS, ROWS, 128), F32), half, ((2, CHUNK, 128), F32)],
        4e9, 12,
        middle, outer, jnp.asarray(y_tables()),
        scratch=[pltpu.VMEM((OUTS, ROWS, 128), F32)],
    )
    devices = lax.axis_size("gx") * lax.axis_size("gy") * lax.axis_size("gz")
    model, sums = call(
        model_kernel,
        [half, ((devices, 128), F32)],
        4e9, 12,
        local, inside_sums, left, right, jnp.asarray(halo_tables()),
        scratch=[
            pltpu.VMEM((256, ROWS), F32),
            pltpu.VMEM((ROWS, OUTS * 128), F32),
            pltpu.VMEM((2, CHUNK, 128), F32),
        ],
    )
    sums = lax.all_to_all(sums, ("gx", "gy", "gz"), 0, 0, tiled=True)
    first, last, to_right, to_left = call(
        send_kernel,
        [((8, COLS), F32), ((8, COLS), F32), ((8, ROWS), F32), ((8, ROWS), F32)],
        1e8, 4,
        model, inside, jnp.asarray(d_edge_tables()),
    )
    left, right = exchange(to_right, to_left, "gy")
    before, after = exchange(last, first, "gx")
    model, inside = call(
        local_kernel,
        [half, half],
        4e9, 8,
        model, inside, jnp.asarray(d_x_tables()), jnp.asarray(d_y_tables()),
        scratch=[pltpu.VMEM((ROWS, COLS), F32)],
        aliases={0: 0, 1: 1},
    )
    field = ((3, ROWS, COLS), F32)
    model, inside = call(
        halo_kernel,
        [half, half],
        1e9, 8,
        model, inside, before, after, left, right, jnp.asarray(d_halo_tables()),
        aliases={0: 0, 1: 1},
    )
    divergence, coefficient = call(
        scale_kernel,
        [field, ((lax.axis_size("gz"),), F32)],
        1e8, 8,
        model, inside, sums,
        out_specs=[VMEM, pl.BlockSpec(memory_space=pltpu.SMEM)],
    )
    return divergence[:, None], coefficient


def solution(mesh):
    return jax.shard_map(
        on_device,
        mesh=mesh,
        in_specs=(P(None, "gz", "gx", "gy"),),
        out_specs=(P(None, "gz", "gx", "gy"), P()),
        check_vma=False,
    )
```
